32 devices in a mesh: ctx: 16 (over z, y, x), tp: 2 (over core).
Axes of the slice: x: 2, y: 2, z: 4, core: 2. Of those that a mesh axis runs over, the one named last changes fastest.
Arguments:
- inputs: bfloat16 [2048, 2048], P('ctx', 'tp'), may hold values from -6.5 to 6.5
- query_weight: bfloat16 [2048, 1024], P(None, 'tp'), may hold values from -0.125 to 0.125
- key_weight: bfloat16 [2048, 1024], P(None, 'tp'), may hold values from -0.125 to 0.125
- value_weight: bfloat16 [2048, 2048], P(None, 'tp'), may hold values from -0.125 to 0.125
- beta_weight: bfloat16 [2048, 16], P(None, 'tp'), may hold values from -1.5 to 1.5
- alpha_weight: bfloat16 [2048, 16], P(None, 'tp'), may hold values from -0.125 to 0.125
- query_filter: bfloat16 [4, 1024], P(None, 'tp'), may hold values from -3 to 3
- key_filter: bfloat16 [4, 1024], P(None, 'tp'), may hold values from -3 to 3
- value_filter: bfloat16 [4, 2048], P(None, 'tp'), may hold values from -3 to 3
- decay_log: float32 [16], P('tp'), may hold values from 0 to 2.77
- step_bias: float32 [16], P('tp'), may hold values from -16 to -2.3
- grad_core: bfloat16 [2048, 2048], P('ctx', 'tp'), may hold values from -6 to 6
Outputs:
- grad_inputs: bfloat16 [2048, 2048], P('ctx', 'tp')
The draws below stay inside these ranges and needn't reach their ends.
All inputs are finite; a program needn't handle non-finite values.
Results may differ from the reference program's by a relative error of at most 0.019.
Values may be sent and summed in bfloat16 or wider, within the bound.
A program may use at most 128 MiB of HBM per device.

```python
import math
import jax
import jax.numpy as jnp
from jax import lax

D = 2048
HK = 8
HV = 16
DH = 128
CONV = 4
GROUP = 64
SEQ = 2048


def head_roles(key):
    order = jax.random.permutation(jax.random.fold_in(key, 7001), HV)
    keeping = HV // 2
    return order < keeping


def mean_signs(key):
    flips = jax.random.randint(jax.random.fold_in(key, 7002), (D,), 0, 2)
    return flips.astype(jnp.float32) - 0.5


def draw_inputs(key, part):
    signs = mean_signs(key)
    noise_key = jax.random.fold_in(key, 7003)
    noise = jax.random.truncated_normal(noise_key, -6.0, 6.0, (SEQ, D), jnp.float32)
    return (noise + signs[None, :]).astype(jnp.bfloat16)


def draw_beta_weight(key, part):
    keeping = head_roles(key)
    signs = mean_signs(key)
    base_key = jax.random.fold_in(key, 7005)
    base = jax.random.truncated_normal(base_key, -6.0, 6.0, (D, HV), jnp.float32)
    target = math.log(0.6 * DH / SEQ)
    slow_cols = base * (0.5 / math.sqrt(D)) + target * 4.0 / D * signs[:, None]
    fast_cols = base * (1.0 / math.sqrt(D))
    return jnp.where(keeping[None, :], slow_cols, fast_cols).astype(jnp.bfloat16)


def draw_decay_log(key, part):
    keeping = head_roles(key)
    spread = jax.random.uniform(jax.random.fold_in(key, 7006), (HV,), jnp.float32, 0.0, 1.0)
    return jnp.where(keeping, 0.3 * spread, 2.77 * spread).astype(jnp.float32)


def draw_step_bias(key, part):
    keeping = head_roles(key)
    spread = jax.random.uniform(jax.random.fold_in(key, 7007), (HV,), jnp.float32, 0.0, 1.0)
    slow_bias = math.log(0.1 / SEQ) - 1.0 + spread
    fast_bias = -7.0 + 4.7 * spread
    return jnp.where(keeping, slow_bias, fast_bias).astype(jnp.float32)


def levels(stream_key, shape, cuts, low, largest):
    def one(dim, blocks):
        steps = jax.random.uniform(jax.random.fold_in(jax.random.fold_in(stream_key, 6), dim), (blocks,), jnp.float32, low / len(cuts), largest / len(cuts))
        return jnp.repeat(jnp.exp(steps), shape[dim] // blocks).reshape((-1,) + (1,) * (len(shape) - dim - 1))

    level = one(*cuts[0])
    for cut in cuts[1:]:
        level = level * one(*cut)
    return level


def centred(rng, extent, deviation, reach, split=(), kind=jnp.bfloat16):
    values = deviation * jax.random.normal(rng, extent, jnp.float32)
    if split:
        values = values * levels(rng, extent, split, -0.22, 0.18)
    return jnp.clip(values, -reach, reach).astype(kind)


def setup_inputs(seed: int = 0) -> dict:
    splits = jax.random.split(jax.random.key(seed), 13)
    inputs = draw_inputs(jax.random.fold_in(splits[12], 71), 0)
    query_weight = centred(splits[1], (D, HK * DH), D ** -0.5, 0.125, ((1, 2),))
    key_weight = centred(splits[2], (D, HK * DH), D ** -0.5, 0.125, ((1, 2),))
    value_weight = centred(splits[3], (D, HV * DH), D ** -0.5, 0.125, ((1, 2),))
    beta_weight = draw_beta_weight(jax.random.fold_in(splits[12], 71), 0)
    alpha_weight = centred(splits[5], (D, HV), D ** -0.5, 0.125, ((1, 2),))
    query_filter = centred(splits[6], (CONV, HK * DH), CONV ** -0.5, 3.0, ((1, 2),))
    key_filter = centred(splits[7], (CONV, HK * DH), CONV ** -0.5, 3.0, ((1, 2),))
    value_filter = centred(splits[8], (CONV, HV * DH), CONV ** -0.5, 3.0, ((1, 2),))
    decay_log = draw_decay_log(jax.random.fold_in(splits[12], 71), 0)
    step_bias = draw_step_bias(jax.random.fold_in(splits[12], 71), 0)
    grad_core = centred(splits[11], (SEQ, HV * DH), 1.0, 6.0, ((0, 16), (1, 2)))
    return dict(inputs=inputs, query_weight=query_weight, key_weight=key_weight, value_weight=value_weight, beta_weight=beta_weight, alpha_weight=alpha_weight, query_filter=query_filter, key_filter=key_filter, value_filter=value_filter, decay_log=decay_log, step_bias=step_bias, grad_core=grad_core)


EPS = 1e-06

def contract(form, left_arr, right_arr):
    return jnp.einsum(form, left_arr, right_arr, precision=lax.Precision.HIGHEST, preferred_element_type=jnp.float32)

def unit_lower_inverse(strict):
    size_now = strict.shape[-1]
    identity = jnp.eye(size_now, dtype=jnp.float32)
    result = identity - strict
    power_of = contract('...ij,...jk->...ik', strict, strict)
    covered = 2
    while covered < size_now:
        result = contract('...ij,...jk->...ik', result, identity + power_of)
        power_of = contract('...ij,...jk->...ik', power_of, power_of)
        covered = covered * 2
    return result

def conv_silu(padded, weight):
    tap_count = weight.shape[0]
    length = padded.shape[0] - tap_count + 1
    running = jnp.zeros((length, padded.shape[1]), jnp.float32)
    for tap_index in range(tap_count):
        running = running + weight[tap_index].astype(jnp.float32) * padded[tap_index:tap_index + length]
    return jax.nn.silu(running)

def normalized(rows_in, heads_count):
    shaped = rows_in.reshape(rows_in.shape[0], heads_count, -1)
    return shaped * lax.rsqrt(lax.optimization_barrier(jnp.sum(shaped * shaped, axis=-1, keepdims=True)) + EPS)

def to_blocks(rows_in, block_count):
    return rows_in.reshape(block_count, GROUP, rows_in.shape[1], -1).transpose(0, 2, 1, 3)

def prepare(query_pad, key_pad, value_pad, beta_raw, alpha_raw, query_filter, key_filter, value_filter, decay_log, step_bias):
    query_act = conv_silu(query_pad, query_filter)
    key_act = conv_silu(key_pad, key_filter)
    value_act = conv_silu(value_pad, value_filter)
    length = query_act.shape[0]
    key_heads = query_act.shape[1] // DH
    value_heads = value_act.shape[1] // DH
    ratio_kv = value_heads // key_heads
    block_count = length // GROUP
    query_unit = jnp.repeat(normalized(query_act, key_heads) * DH ** (-0.5), ratio_kv, axis=1)
    key_unit = jnp.repeat(normalized(key_act, key_heads), ratio_kv, axis=1)
    query_blk = to_blocks(query_unit, block_count)
    key_blk = to_blocks(key_unit, block_count)
    value_blk = to_blocks(value_act.reshape(length, value_heads, DH), block_count)
    beta_blk = jax.nn.sigmoid(beta_raw).reshape(block_count, GROUP, value_heads).transpose(0, 2, 1)
    log_decay = -jnp.exp(decay_log) * jax.nn.softplus(alpha_raw + step_bias)
    cum_decay = jnp.cumsum(log_decay.reshape(block_count, GROUP, value_heads).transpose(0, 2, 1), axis=-1)
    row_pos = lax.broadcasted_iota(jnp.int32, (GROUP, GROUP), 0)
    col_pos = lax.broadcasted_iota(jnp.int32, (GROUP, GROUP), 1)
    lower_mask = row_pos >= col_pos
    strictly = row_pos > col_pos
    gap_log = cum_decay[..., :, None] - cum_decay[..., None, :]
    decay_ij = jnp.where(lower_mask, jnp.exp(jnp.where(lower_mask, gap_log, 0.0)), 0.0)
    key_gram = contract('nhia,nhja->nhij', key_blk, key_blk)
    strict = jnp.where(strictly, beta_blk[..., :, None] * key_gram * decay_ij, 0.0)
    inverse = unit_lower_inverse(strict)
    gamma_at = jnp.exp(cum_decay)
    value_mix = contract('nhij,nhjb->nhib', inverse, beta_blk[..., None] * value_blk)
    key_weighted = contract('nhij,nhja->nhia', inverse, (beta_blk * gamma_at)[..., None] * key_blk)
    query_scaled = gamma_at[..., None] * query_blk
    key_tail = jnp.exp(cum_decay[..., -1:] - cum_decay)[..., None] * key_blk
    mixing = contract('nhia,nhja->nhij', query_blk, key_blk) * decay_ij
    end_decay = jnp.exp(cum_decay[..., -1])
    return (query_scaled, key_weighted, value_mix, key_tail, mixing, end_decay)

def transitions(pieces):
    query_scaled, key_weighted, value_mix, key_tail, mixing, end_decay = pieces
    unit_matrix = jnp.eye(key_tail.shape[-1], dtype=jnp.float32)
    trans_step = end_decay[..., None, None] * unit_matrix - contract('nhca,nhcd->nhad', key_tail, key_weighted)
    inject_step = contract('nhca,nhcb->nhab', key_tail, value_mix)
    return (trans_step, inject_step)

def head_outputs(pieces, starts):
    query_scaled, key_weighted, value_mix, key_tail, mixing, end_decay = pieces
    fresh = value_mix - contract('nhca,nhab->nhcb', key_weighted, starts)
    return contract('nhca,nhab->nhcb', query_scaled, starts) + contract('nhij,nhjb->nhib', mixing, fresh)

def core_forward(proj_query, proj_key, proj_value, proj_beta, proj_alpha, query_filter, key_filter, value_filter, decay_log, step_bias):
    conv_lag = CONV - 1

    def front_pad(rows_in):
        return jnp.concatenate([jnp.zeros((conv_lag, rows_in.shape[1]), jnp.float32), rows_in], 0)
    pieces = prepare(front_pad(proj_query), front_pad(proj_key), front_pad(proj_value), proj_beta, proj_alpha, query_filter, key_filter, value_filter, decay_log, step_bias)
    trans_step, inject_step = transitions(pieces)

    def advance(carried, step_pair):
        return (contract('had,hdb->hab', step_pair[0], carried) + step_pair[1], carried)
    initial = jnp.zeros(inject_step.shape[1:], jnp.float32)
    _, starts = lax.scan(advance, initial, (trans_step, inject_step))
    heads_out = head_outputs(pieces, starts)
    return heads_out.transpose(0, 2, 1, 3).reshape(proj_query.shape[0], -1)

def reference(inputs, query_weight, key_weight, value_weight, beta_weight, alpha_weight, query_filter, key_filter, value_filter, decay_log, step_bias, grad_core):
    weights = (query_weight, key_weight, value_weight, beta_weight, alpha_weight)
    rounded = lax.optimization_barrier(tuple((jnp.dot(inputs, weight, preferred_element_type=jnp.float32).astype(jnp.bfloat16) for weight in weights)))
    primals = tuple((member.astype(jnp.float32) for member in rounded))

    def forward(proj_query, proj_key, proj_value, proj_beta, proj_alpha):
        return core_forward(proj_query, proj_key, proj_value, proj_beta, proj_alpha, query_filter, key_filter, value_filter, decay_log, step_bias)
    _, backward = jax.vjp(forward, *primals)
    gradients = backward(grad_core.astype(jnp.float32))
    running = jnp.zeros(inputs.shape, jnp.float32)
    for grad_rows, weight in zip(gradients, weights):
        running = running + lax.dot_general(grad_rows.astype(jnp.bfloat16), weight, (((1,), (1,)), ((), ())), preferred_element_type=jnp.float32)
    return running.astype(jnp.bfloat16)
```

```python
import functools

import jax
import jax.numpy as jnp
from jax import lax
from jax.experimental import pallas as pl
from jax.experimental.pallas import tpu as pltpu
from jax.sharding import PartitionSpec as P

DH = 128
CONV = 4
EPS = 1e-06
MESH = pl.DeviceIdType.MESH
BF = jnp.bfloat16
F32 = jnp.float32


def mm(left, right, lc, rc):
    return lax.dot_general(
        left.astype(BF), right.astype(BF), (((lc,), (rc,)), ((), ())), preferred_element_type=F32
    )


def nn(left, right):
    return mm(left, right, 1, 0)


def nt(left, right):
    return mm(left, right, 1, 1)


def tn(left, right):
    return mm(left, right, 0, 0)


def rowsum(value):
    return jnp.sum(value, axis=1, keepdims=True)


def colsum(value):
    return jnp.sum(value, axis=0, keepdims=True)


def column(ref, head):
    value = ref[...]
    lanes = lax.broadcasted_iota(jnp.int32, value.shape, 1)
    return rowsum(jnp.where(lanes == head, value, 0.0))


def lane_block(head):
    return pl.ds(pl.multiple_of(head * DH, DH), DH)


def inverses(stricts):
    size = stricts[0].shape[0]
    row = lax.broadcasted_iota(jnp.int32, (size, size), 0)
    col = lax.broadcasted_iota(jnp.int32, (size, size), 1)
    results = [jnp.where(row == col, 1.0, 0.0) - jnp.where((row // 2) == (col // 2), a, 0.0) for a in stricts]
    block = 2
    while block < size:
        within = ((row // (2 * block)) == (col // (2 * block))) & ((row // block) > (col // block))
        parts = [jnp.where(within, a, 0.0) for a in stricts]
        halves = [nn(a, m) for a, m in zip(parts, results)]
        results = [m - nn(m, a) for m, a in zip(results, halves)]
        block *= 2
    return results


def core_kernel(
    kheads, ratio, group,
    q_ref, k_ref, v_ref, beta_ref, gc_ref, gr_ref, do_ref,
    dq_ref, dk_ref, dv_ref, dbeta_ref, dgc_ref, dgr_ref,
    inv_s, w_s, vm_s, y_s, move_s, add_s, end_s, land_s, out_s,
    send_sem, recv_sem,
):
    count, me = lax.axis_size("ctx"), lax.axis_index("ctx")
    vheads = kheads * ratio
    size = q_ref.shape[0]
    row = lax.broadcasted_iota(jnp.int32, (size, size), 0)
    col = lax.broadcasted_iota(jnp.int32, (size, size), 1)
    lower, strictly = row >= col, row > col

    barrier = pltpu.get_barrier_semaphore()

    @pl.when(me > 0)
    def _():
        pl.semaphore_signal(barrier, inc=1, device_id={"ctx": me - 1}, device_id_type=MESH)

    @pl.when(me < count - 1)
    def _():
        pl.semaphore_signal(barrier, inc=1, device_id={"ctx": me + 1}, device_id_type=MESH)

    def gates(head):
        gc, gr = column(gc_ref, head), gr_ref[pl.ds(head, 1), :]
        decay = jnp.where(lower, jnp.exp(jnp.where(lower, gc - gr, 0.0)), 0.0)
        last = gc[size - 1 : size, :]
        return column(beta_ref, head), decay, jnp.exp(gc), jnp.exp(last - gc), jnp.exp(last)

    def prepare(step, carry):
        kh = [step * group + i for i in range(group)]
        ks = [k_ref[:, lane_block(h)] for h in kh]
        qs = [q_ref[:, lane_block(h)] for h in kh]
        kk = [nt(k, k) for k in ks]
        qk = [nt(q, k) for q, k in zip(qs, ks)]
        heads = [(i, kh[i] * ratio + r) for i in range(group) for r in range(ratio)]
        gate = [gates(h) for _, h in heads]
        stricts = [
            jnp.where(strictly, g[0] * kk[i] * g[1], 0.0) for (i, _), g in zip(heads, gate)
        ]
        invs = inverses(stricts)
        dos = [do_ref[:, lane_block(h)] for _, h in heads]
        ys = [tn(qk[i] * g[1], do) for (i, _), g, do in zip(heads, gate, dos)]
        ws = [nn(m, (g[0] * g[2]) * ks[i]) for (i, _), g, m in zip(heads, gate, invs)]
        vms = [nn(m, g[0] * v_ref[:, lane_block(h)]) for (_, h), g, m in zip(heads, gate, invs)]
        kts = [g[3] * ks[i] for (i, _), g in zip(heads, gate)]
        for n, (i, h) in enumerate(heads):
            inv_s[h] = invs[n].astype(BF)
            w_s[h] = ws[n].astype(BF)
            vm_s[h] = vms[n]
            y_s[h] = ys[n]
            end_s[h] = jnp.broadcast_to(gate[n][4], (8, DH))
            move_s[0, h] = tn(kts[n], ws[n]).astype(BF)
            move_s[1, h] = tn(ws[n], kts[n]).astype(BF)
            add_s[0, h] = tn(kts[n], vms[n])
            add_s[1, h] = tn(gate[n][2] * qs[i], dos[n]) - tn(ws[n], ys[n])
        return carry

    lax.fori_loop(0, kheads // group, prepare, 0)

    peers = jnp.minimum(me, 1) + jnp.minimum(count - 1 - me, 1)
    pl.semaphore_wait(barrier, peers)

    @pl.when(me == 0)
    def _():
        land_s[0] = jnp.zeros(land_s.shape[1:], land_s.dtype)

    @pl.when(me == count - 1)
    def _():
        land_s[1] = jnp.zeros(land_s.shape[1:], land_s.dtype)

    late = (2 * me) // count

    def hop(way, head, target):
        return pltpu.make_async_remote_copy(
            src_ref=out_s.at[way, head],
            dst_ref=land_s.at[way, head],
            send_sem=send_sem.at[way, head],
            recv_sem=recv_sem.at[way, head],
            device_id={"ctx": target},
            device_id_type=MESH,
        )

    def chain(step, carry):
        turn, head = step // vheads, step % vheads
        way = turn + late - 2 * turn * late
        before, after = me - 1 + 2 * way, me + 1 - 2 * way

        @pl.when((before >= 0) & (before < count))
        def _():
            hop(way, head, before).wait_recv()

        @pl.when((after >= 0) & (after < count))
        def _():
            state = land_s[way, head]
            out_s[way, head] = (
                end_s[head][0:1, :] * state.astype(F32)
                - nn(move_s[way, head], state)
                + add_s[way, head]
            ).astype(BF)
            hop(way, head, after).start()

        return carry

    lax.fori_loop(0, 2 * vheads, chain, 0)

    dbeta_ref[...] = jnp.zeros(dbeta_ref.shape, F32)
    dgc_ref[...] = jnp.zeros(dgc_ref.shape, F32)
    gate_lanes = lax.broadcasted_iota(jnp.int32, dbeta_ref.shape, 1)
    at_end = lax.broadcasted_iota(jnp.int32, (size, 1), 0) == size - 1

    def back(step, carry):
        kh = [step * group + i for i in range(group)]
        ks = [k_ref[:, lane_block(h)] for h in kh]
        qs = [q_ref[:, lane_block(h)] for h in kh]
        kk = [nt(k, k) for k in ks]
        qk = [nt(q, k) for q, k in zip(qs, ks)]
        heads = [(i, kh[i] * ratio + r) for i in range(group) for r in range(ratio)]
        span = range(len(heads))
        gate = [gates(h) for _, h in heads]
        own_k = [ks[i] for i, _ in heads]
        own_q = [qs[i] for i, _ in heads]
        dos = [do_ref[:, lane_block(h)] for _, h in heads]
        vs = [v_ref[:, lane_block(h)] for _, h in heads]
        starts = [land_s[0, h] for _, h in heads]
        ends = [land_s[1, h] for _, h in heads]
        fresh = [vm_s[h] - nn(w_s[h], starts[n]) for n, (_, h) in enumerate(heads)]
        xs = [nn(own_k[n], starts[n]) for n in span]
        dfresh = [
            y_s[h] + nn(gate[n][3] * own_k[n], ends[n]) for n, (_, h) in enumerate(heads)
        ]
        drs = [tn(inv_s[h], dfresh[n]) for n, (_, h) in enumerate(heads)]
        dps = [nt(dos[n], fresh[n]) for n in span]
        dqs = [nt(dos[n], starts[n]) for n in span]
        dkt = [nt(fresh[n], ends[n]) for n in span]
        das = [jnp.where(strictly, -nt(drs[n], fresh[n]), 0.0) for n in span]
        dxs = [nt((gate[n][0] * gate[n][2]) * drs[n], starts[n]) for n in span]
        dqk = [0.0] * group
        dkk = [0.0] * group
        dq = [0.0] * group
        dk = [0.0] * group
        for n, (i, h) in enumerate(heads):
            beta, decay, gam, tail, end = gate[n]
            k, q = own_k[n], own_q[n]
            dpd = dps[n] * decay
            dad = das[n] * decay
            dad_kk = dad * kk[i]
            dqk[i] += dpd
            dkk[i] += beta * dad
            logs = dpd * qk[i] + beta * dad_kk
            dgam = rowsum(q * dqs[n]) - beta * rowsum(drs[n] * xs[n])
            dtail = rowsum(k * dkt[n]) * tail
            dend = jnp.sum(
                starts[n].astype(F32) * ends[n].astype(F32), axis=(0, 1), keepdims=True
            ) * end
            dbeta = rowsum(drs[n] * (vs[n] - gam * xs[n])) + rowsum(dad_kk)
            dgc = rowsum(logs) + dgam * gam - dtail
            dgc += jnp.where(at_end, colsum(dtail) + dend, 0.0)
            dq[i] += gam * dqs[n]
            dk[i] += tail * dkt[n] - dxs[n]
            dv_ref[:, lane_block(h)] = beta * drs[n]
            dbeta_ref[...] += jnp.where(gate_lanes == h, dbeta, 0.0)
            dgc_ref[...] += jnp.where(gate_lanes == h, dgc, 0.0)
            dgr_ref[pl.ds(h, 1), :] = -colsum(logs)
        for i in range(group):
            dq_ref[:, lane_block(kh[i])] = dq[i] + nn(dqk[i], ks[i])
            dk_ref[:, lane_block(kh[i])] = (
                dk[i] + tn(dqk[i], qs[i]) + nn(dkk[i], ks[i]) + tn(dkk[i], ks[i])
            )
        return carry

    lax.fori_loop(0, kheads // group, back, 0)

    def drain(head, carry):
        @pl.when(me < count - 1)
        def _():
            hop(0, head, me + 1).wait_send()

        @pl.when(me > 0)
        def _():
            hop(1, head, me - 1).wait_send()

        return carry

    lax.fori_loop(0, vheads, drain, 0)


def recurrence_grads(q, k, v, beta, gc, gr, grad_core):
    size = q.shape[0]
    kheads, vheads = q.shape[1] // DH, v.shape[1] // DH
    ratio = vheads // kheads
    group = 2 if kheads % 2 == 0 else 1
    shapes = [q, k, v, beta, gc, gr]
    square = (DH, DH)
    vmem = pl.BlockSpec(memory_space=pltpu.VMEM)
    return pl.pallas_call(
        functools.partial(core_kernel, kheads, ratio, group),
        out_shape=[jax.ShapeDtypeStruct(a.shape, F32) for a in shapes],
        in_specs=[vmem] * 7,
        out_specs=[vmem] * 6,
        scratch_shapes=[
            pltpu.VMEM((vheads, size, size), BF),
            pltpu.VMEM((vheads, size, DH), BF),
            pltpu.VMEM((vheads, size, DH), F32),
            pltpu.VMEM((vheads, size, DH), F32),
            pltpu.VMEM((2, vheads) + square, BF),
            pltpu.VMEM((2, vheads) + square, F32),
            pltpu.VMEM((vheads, 8, DH), F32),
            pltpu.VMEM((2, vheads) + square, BF),
            pltpu.VMEM((2, vheads) + square, BF),
            pltpu.SemaphoreType.DMA((2, vheads)),
            pltpu.SemaphoreType.DMA((2, vheads)),
        ],
        compiler_params=pltpu.CompilerParams(
            collective_id=0, has_side_effects=True, vmem_limit_bytes=40 * 1024 * 1024
        ),
    )(q, k, v, beta, gc, gr, grad_core)


def from_behind(value, axis, steps):
    count = lax.axis_size(axis)
    leading, last = (max(0, -steps), min(count, count - steps))
    return lax.ppermute(value, axis, [(source, source + steps) for source in range(leading, last)])


def conv_silu(padded, weight):
    tap_count = weight.shape[0]
    length = padded.shape[0] - tap_count + 1
    running = jnp.zeros((length, padded.shape[1]), F32)
    for tap in range(tap_count):
        running = running + weight[tap].astype(F32) * padded[tap : tap + length]
    return jax.nn.silu(running)


def normalized(rows_in, scale):
    shaped = rows_in.reshape(rows_in.shape[0], -1, DH)
    unit = shaped * (lax.rsqrt(jnp.sum(shaped * shaped, axis=-1, keepdims=True) + EPS) * scale)
    return unit.reshape(rows_in.shape)


def running_sum(log_decay):
    size = log_decay.shape[0]
    row = lax.broadcasted_iota(jnp.int32, (size, size), 0)
    col = lax.broadcasted_iota(jnp.int32, (size, size), 1)
    return jnp.dot(
        jnp.where(row >= col, 1.0, 0.0), log_decay, precision=lax.Precision.HIGHEST,
        preferred_element_type=F32,
    )


def local(
    inputs, query_weight, key_weight, value_weight, beta_weight, alpha_weight,
    query_filter, key_filter, value_filter, decay_log, step_bias, grad_core,
):
    rows_here = inputs.shape[0]
    lag = CONV - 1
    weights = (query_weight, key_weight, value_weight, beta_weight, alpha_weight)
    pair = lax.axis_size("tp") == 2
    side = lax.axis_index("tp")
    if pair:
        other = lax.ppermute(inputs, "tp", [(0, 1), (1, 0)])
        whole = jnp.where(
            side == 0,
            jnp.concatenate([inputs, other], 1),
            jnp.concatenate([other, inputs], 1),
        )
    else:
        whole = lax.all_gather(inputs, "tp", axis=1, tiled=True)
    rounded = lax.optimization_barrier(
        tuple(jnp.dot(whole, w, preferred_element_type=F32).astype(BF) for w in weights)
    )
    tails = from_behind(
        jnp.concatenate([m[rows_here - lag :] for m in rounded[:3]], 1), "ctx", 1
    )
    widths = [m.shape[1] for m in rounded[:3]]
    cuts = [0, widths[0], widths[0] + widths[1], sum(widths)]
    tails = [tails[:, cuts[n] : cuts[n + 1]] for n in range(3)]
    padded = [jnp.concatenate([t, m], 0).astype(F32) for t, m in zip(tails, rounded)]

    def front(query_pad, key_pad, value_pad, beta_raw, alpha_raw):
        q = normalized(conv_silu(query_pad, query_filter), DH ** (-0.5))
        k = normalized(conv_silu(key_pad, key_filter), 1.0)
        v = conv_silu(value_pad, value_filter)
        beta = jax.nn.sigmoid(beta_raw)
        log_decay = -jnp.exp(decay_log) * jax.nn.softplus(alpha_raw + step_bias)
        return q, k, v, beta, running_sum(log_decay)

    (q, k, v, beta, gc), front_back = jax.vjp(
        front, *padded, rounded[3].astype(F32), rounded[4].astype(F32)
    )
    dq, dk, dv, dbeta, dgc, dgr = recurrence_grads(q, k, v, beta, gc, gc.T, grad_core)
    grads = front_back((dq, dk, dv, dbeta, dgc + dgr.T))
    arriving = from_behind(jnp.concatenate([g[:lag] for g in grads[:3]], 1), "ctx", -1)
    full = []
    for n in range(3):
        tail = arriving[:, cuts[n] : cuts[n + 1]]
        full.append((grads[n][lag:] + jnp.pad(tail, ((rows_here - lag, 0), (0, 0)))).astype(BF))
    full += [g.astype(BF) for g in grads[3:]]

    def contribution(pieces):
        total = 0.0
        for grad_rows, weight in zip(full, pieces):
            total = total + lax.dot_general(
                grad_rows, weight, (((1,), (1,)), ((), ())), preferred_element_type=F32
            )
        return total

    share = inputs.shape[1]
    if pair:
        far = contribution(
            [lax.dynamic_slice_in_dim(w, (1 - side) * share, share, 0) for w in weights]
        ).astype(BF)
        arrived = lax.ppermute(far, "tp", [(0, 1), (1, 0)])
        near = contribution(
            [lax.dynamic_slice_in_dim(w, side * share, share, 0) for w in weights]
        )
        return (near + arrived.astype(F32)).astype(BF)
    return lax.psum_scatter(
        contribution(weights).astype(BF), "tp", scatter_dimension=1, tiled=True
    )


def solution(mesh):
    return jax.shard_map(
        local,
        mesh=mesh,
        in_specs=(
            P("ctx", "tp"),
            P(None, "tp"),
            P(None, "tp"),
            P(None, "tp"),
            P(None, "tp"),
            P(None, "tp"),
            P(None, "tp"),
            P(None, "tp"),
            P(None, "tp"),
            P("tp"),
            P("tp"),
            P("ctx", "tp"),
        ),
        out_specs=P("ctx", "tp"),
        check_vma=False,
    )
```

```python
import functools

import jax
import jax.numpy as jnp
from jax import lax
from jax.experimental import pallas as pl
from jax.experimental.pallas import tpu as pltpu
from jax.sharding import PartitionSpec as P

DH = 128
CONV = 4
EPS = 1e-06
MESH = pl.DeviceIdType.MESH
BF = jnp.bfloat16
F32 = jnp.float32


def mm(left, right, lc, rc):
    return lax.dot_general(
        left.astype(BF), right.astype(BF), (((lc,), (rc,)), ((), ())), preferred_element_type=F32
    )


def nn(left, right):
    return mm(left, right, 1, 0)


def nt(left, right):
    return mm(left, right, 1, 1)


def tn(left, right):
    return mm(left, right, 0, 0)


def rowsum(value):
    return jnp.sum(value, axis=1, keepdims=True)


def colsum(value):
    return jnp.sum(value, axis=0, keepdims=True)


def column(ref, head):
    value = ref[...]
    lanes = lax.broadcasted_iota(jnp.int32, value.shape, 1)
    return rowsum(jnp.where(lanes == head, value, 0.0))


def lane_block(head):
    return pl.ds(pl.multiple_of(head * DH, DH), DH)


def inverses(stricts):
    size = stricts[0].shape[0]
    row = lax.broadcasted_iota(jnp.int32, (size, size), 0)
    col = lax.broadcasted_iota(jnp.int32, (size, size), 1)
    results = [jnp.where(row == col, 1.0, 0.0) - jnp.where((row // 2) == (col // 2), a, 0.0) for a in stricts]
    block = 2
    while block < size:
        within = ((row // (2 * block)) == (col // (2 * block))) & ((row // block) > (col // block))
        parts = [jnp.where(within, a, 0.0) for a in stricts]
        halves = [nn(a, m) for a, m in zip(parts, results)]
        results = [m - nn(m, a) for m, a in zip(results, halves)]
        block *= 2
    return results


def core_kernel(
    kheads, ratio, group,
    pq_ref, pk_ref, pv_ref, taps_ref, beta_ref, gc_ref, gr_ref, do_ref,
    dpq_ref, dpk_ref, dpv_ref, dbeta_ref, dgc_ref, dgr_ref,
    q_ref, k_ref, v_ref, pad_s, run_s, dpad_s, tail_s, tail_land, dtail_land,
    tail_sems, inv_s, w_s, vm_s, y_s, move_s, add_s, end_s, land_s, out_s,
    send_sem, recv_sem,
):
    count, me = lax.axis_size("ctx"), lax.axis_index("ctx")
    vheads = kheads * ratio
    size = pq_ref.shape[0]
    kw, vw = pq_ref.shape[1], pv_ref.shape[1]
    width = 2 * kw + vw
    projected = ((pq_ref, 0, kw), (pk_ref, kw, kw), (pv_ref, 2 * kw, vw))
    row = lax.broadcasted_iota(jnp.int32, (size, size), 0)
    col = lax.broadcasted_iota(jnp.int32, (size, size), 1)
    lower, strictly = row >= col, row > col

    barrier = pltpu.get_barrier_semaphore()

    @pl.when(me > 0)
    def _():
        pl.semaphore_signal(barrier, inc=1, device_id={"ctx": me - 1}, device_id_type=MESH)

    @pl.when(me < count - 1)
    def _():
        pl.semaphore_signal(barrier, inc=1, device_id={"ctx": me + 1}, device_id_type=MESH)

    peers = jnp.minimum(me, 1) + jnp.minimum(count - 1 - me, 1)
    pl.semaphore_wait(barrier, peers)

    def tail_copy():
        return pltpu.make_async_remote_copy(
            src_ref=tail_s, dst_ref=tail_land, send_sem=tail_sems.at[0], recv_sem=tail_sems.at[1],
            device_id={"ctx": me + 1}, device_id_type=MESH,
        )

    def dtail_copy():
        return pltpu.make_async_remote_copy(
            src_ref=dpad_s.at[0:8], dst_ref=dtail_land, send_sem=tail_sems.at[2],
            recv_sem=tail_sems.at[3], device_id={"ctx": me - 1}, device_id_type=MESH,
        )

    for ref, at, wide in projected:
        tail_s[:, at : at + wide] = ref[size - 16 : size, :]

    @pl.when(me < count - 1)
    def _():
        tail_copy().start()

    for ref, at, wide in projected:
        pad_s[16 : 16 + size, at : at + wide] = ref[...].astype(F32)
    run_s[0:8, :] = jnp.zeros((8, width), F32)
    run_s[8 + size : 16 + size, :] = jnp.zeros((8, width), F32)

    @pl.when(me == 0)
    def _():
        tail_land[...] = jnp.zeros(tail_land.shape, tail_land.dtype)

    @pl.when(me == count - 1)
    def _():
        dtail_land[...] = jnp.zeros(dtail_land.shape, dtail_land.dtype)

    @pl.when(me > 0)
    def _():
        tail_copy().wait_recv()

    pad_s[0:16, :] = tail_land[...].astype(F32)

    def convolved(block):
        lanes = lane_block(block)
        taps = taps_ref[:, lanes]
        total = taps[0:1, :] * pad_s[16 - CONV + 1 : 16 - CONV + 1 + size, lanes]
        for tap in range(1, CONV):
            first = 16 - CONV + 1 + tap
            total += taps[tap : tap + 1, :] * pad_s[first : first + size, lanes]
        gate = 1.0 / (1.0 + jnp.exp(-total))
        return total, gate

    def unit(act):
        return lax.rsqrt(rowsum(act * act) + EPS)

    def front_qk(head, carry):
        for ref, first, scale in ((q_ref, 0, DH ** (-0.5)), (k_ref, kheads, 1.0)):
            total, gate = convolved(first + head)
            act = total * gate
            ref[:, lane_block(head)] = act * (unit(act) * scale)
        return carry

    def front_v(head, carry):
        total, gate = convolved(2 * kheads + head)
        v_ref[:, lane_block(head)] = total * gate
        return carry

    lax.fori_loop(0, kheads, front_qk, 0)
    lax.fori_loop(0, vheads, front_v, 0)

    def front_back(block, grad, scale):
        total, gate = convolved(block)
        if scale is not None:
            act = total * gate
            length = unit(act)
            grad = (scale * length) * (grad - act * (length * length * rowsum(act * grad)))
        run_s[8 : 8 + size, lane_block(block)] = grad * (gate * (1.0 + total * (1.0 - gate)))

    def gates(head):
        gc, gr = column(gc_ref, head), gr_ref[pl.ds(head, 1), :]
        decay = jnp.where(lower, jnp.exp(jnp.where(lower, gc - gr, 0.0)), 0.0)
        last = gc[size - 1 : size, :]
        return column(beta_ref, head), decay, jnp.exp(gc), jnp.exp(last - gc), jnp.exp(last)

    def prepare(step, carry):
        kh = [step * group + i for i in range(group)]
        ks = [k_ref[:, lane_block(h)] for h in kh]
        qs = [q_ref[:, lane_block(h)] for h in kh]
        kk = [nt(k, k) for k in ks]
        qk = [nt(q, k) for q, k in zip(qs, ks)]
        heads = [(i, kh[i] * ratio + r) for i in range(group) for r in range(ratio)]
        gate = [gates(h) for _, h in heads]
        stricts = [
            jnp.where(strictly, g[0] * kk[i] * g[1], 0.0) for (i, _), g in zip(heads, gate)
        ]
        invs = inverses(stricts)
        dos = [do_ref[:, lane_block(h)] for _, h in heads]
        ys = [tn(qk[i] * g[1], do) for (i, _), g, do in zip(heads, gate, dos)]
        ws = [nn(m, (g[0] * g[2]) * ks[i]) for (i, _), g, m in zip(heads, gate, invs)]
        vms = [nn(m, g[0] * v_ref[:, lane_block(h)]) for (_, h), g, m in zip(heads, gate, invs)]
        kts = [g[3] * ks[i] for (i, _), g in zip(heads, gate)]
        for n, (i, h) in enumerate(heads):
            inv_s[h] = invs[n].astype(BF)
            w_s[h] = ws[n].astype(BF)
            vm_s[h] = vms[n]
            y_s[h] = ys[n]
            end_s[h] = jnp.broadcast_to(gate[n][4], (8, DH))
            move_s[0, h] = tn(kts[n], ws[n]).astype(BF)
            move_s[1, h] = tn(ws[n], kts[n]).astype(BF)
            add_s[0, h] = tn(kts[n], vms[n])
            add_s[1, h] = tn(gate[n][2] * qs[i], dos[n]) - tn(ws[n], ys[n])
        return carry

    lax.fori_loop(0, kheads // group, prepare, 0)

    @pl.when(me == 0)
    def _():
        land_s[0] = jnp.zeros(land_s.shape[1:], land_s.dtype)

    @pl.when(me == count - 1)
    def _():
        land_s[1] = jnp.zeros(land_s.shape[1:], land_s.dtype)

    late = (2 * me) // count

    def hop(way, head, target):
        return pltpu.make_async_remote_copy(
            src_ref=out_s.at[way, head],
            dst_ref=land_s.at[way, head],
            send_sem=send_sem.at[way, head],
            recv_sem=recv_sem.at[way, head],
            device_id={"ctx": target},
            device_id_type=MESH,
        )

    def chain(step, carry):
        turn, head = step // vheads, step % vheads
        way = turn + late - 2 * turn * late
        before, after = me - 1 + 2 * way, me + 1 - 2 * way

        @pl.when((before >= 0) & (before < count))
        def _():
            hop(way, head, before).wait_recv()

        @pl.when((after >= 0) & (after < count))
        def _():
            state = land_s[way, head]
            out_s[way, head] = (
                end_s[head][0:1, :] * state.astype(F32)
                - nn(move_s[way, head], state)
                + add_s[way, head]
            ).astype(BF)
            hop(way, head, after).start()

        return carry

    lax.fori_loop(0, 2 * vheads, chain, 0)

    dbeta_ref[...] = jnp.zeros(dbeta_ref.shape, F32)
    dgc_ref[...] = jnp.zeros(dgc_ref.shape, F32)
    gate_lanes = lax.broadcasted_iota(jnp.int32, dbeta_ref.shape, 1)
    at_end = lax.broadcasted_iota(jnp.int32, (size, 1), 0) == size - 1

    def back(step, carry):
        kh = [step * group + i for i in range(group)]
        ks = [k_ref[:, lane_block(h)] for h in kh]
        qs = [q_ref[:, lane_block(h)] for h in kh]
        kk = [nt(k, k) for k in ks]
        qk = [nt(q, k) for q, k in zip(qs, ks)]
        heads = [(i, kh[i] * ratio + r) for i in range(group) for r in range(ratio)]
        span = range(len(heads))
        gate = [gates(h) for _, h in heads]
        own_k = [ks[i] for i, _ in heads]
        own_q = [qs[i] for i, _ in heads]
        dos = [do_ref[:, lane_block(h)] for _, h in heads]
        vs = [v_ref[:, lane_block(h)] for _, h in heads]
        starts = [land_s[0, h] for _, h in heads]
        ends = [land_s[1, h] for _, h in heads]
        fresh = [vm_s[h] - nn(w_s[h], starts[n]) for n, (_, h) in enumerate(heads)]
        xs = [nn(own_k[n], starts[n]) for n in span]
        dfresh = [
            y_s[h] + nn(gate[n][3] * own_k[n], ends[n]) for n, (_, h) in enumerate(heads)
        ]
        drs = [tn(inv_s[h], dfresh[n]) for n, (_, h) in enumerate(heads)]
        dps = [nt(dos[n], fresh[n]) for n in span]
        dqs = [nt(dos[n], starts[n]) for n in span]
        dkt = [nt(fresh[n], ends[n]) for n in span]
        das = [jnp.where(strictly, -nt(drs[n], fresh[n]), 0.0) for n in span]
        dxs = [nt((gate[n][0] * gate[n][2]) * drs[n], starts[n]) for n in span]
        dqk = [0.0] * group
        dkk = [0.0] * group
        dq = [0.0] * group
        dk = [0.0] * group
        for n, (i, h) in enumerate(heads):
            beta, decay, gam, tail, end = gate[n]
            k, q = own_k[n], own_q[n]
            dpd = dps[n] * decay
            dad = das[n] * decay
            dad_kk = dad * kk[i]
            dqk[i] += dpd
            dkk[i] += beta * dad
            logs = dpd * qk[i] + beta * dad_kk
            dgam = rowsum(q * dqs[n]) - beta * rowsum(drs[n] * xs[n])
            dtail = rowsum(k * dkt[n]) * tail
            dend = jnp.sum(
                starts[n].astype(F32) * ends[n].astype(F32), axis=(0, 1), keepdims=True
            ) * end
            dbeta = rowsum(drs[n] * (vs[n] - gam * xs[n])) + rowsum(dad_kk)
            dgc = rowsum(logs) + dgam * gam - dtail
            dgc += jnp.where(at_end, colsum(dtail) + dend, 0.0)
            dq[i] += gam * dqs[n]
            dk[i] += tail * dkt[n] - dxs[n]
            front_back(2 * kheads + h, beta * drs[n], None)
            dbeta_ref[...] += jnp.where(gate_lanes == h, dbeta, 0.0)
            dgc_ref[...] += jnp.where(gate_lanes == h, dgc, 0.0)
            dgr_ref[pl.ds(h, 1), :] = -colsum(logs)
        for i in range(group):
            front_back(kh[i], dq[i] + nn(dqk[i], ks[i]), DH ** (-0.5))
            front_back(
                kheads + kh[i],
                dk[i] + tn(dqk[i], qs[i]) + nn(dkk[i], ks[i]) + tn(dkk[i], ks[i]),
                1.0,
            )
        return carry

    lax.fori_loop(0, kheads // group, back, 0)

    def transposed(block, carry):
        lanes = lane_block(block)
        taps = taps_ref[:, lanes]
        total = taps[0:1, :] * run_s[CONV - 1 : CONV + 7 + size, lanes]
        for tap in range(1, CONV):
            first = CONV - 1 - tap
            total += taps[tap : tap + 1, :] * run_s[first : first + 8 + size, lanes]
        dpad_s[:, lanes] = total
        return carry

    lax.fori_loop(0, width // DH, transposed, 0)

    @pl.when(me > 0)
    def _():
        dtail_copy().start()

    cut = size - 16
    for ref, at, wide in ((dpq_ref, 0, kw), (dpk_ref, kw, kw), (dpv_ref, 2 * kw, vw)):
        ref[0:cut, :] = dpad_s[8 : 8 + cut, at : at + wide].astype(BF)

    @pl.when(me < count - 1)
    def _():
        dtail_copy().wait_recv()

    for ref, at, wide in ((dpq_ref, 0, kw), (dpk_ref, kw, kw), (dpv_ref, 2 * kw, vw)):
        ref[cut:size, :] = jnp.concatenate(
            [
                dpad_s[8 + cut : size, at : at + wide],
                dpad_s[size : 8 + size, at : at + wide] + dtail_land[:, at : at + wide],
            ],
            0,
        ).astype(BF)

    @pl.when(me < count - 1)
    def _():
        tail_copy().wait_send()

    @pl.when(me > 0)
    def _():
        dtail_copy().wait_send()

    def drain(head, carry):
        @pl.when(me < count - 1)
        def _():
            hop(0, head, me + 1).wait_send()

        @pl.when(me > 0)
        def _():
            hop(1, head, me - 1).wait_send()

        return carry

    lax.fori_loop(0, vheads, drain, 0)


def recurrence_grads(q, k, v, taps, beta, gc, gr, grad_core):
    size = q.shape[0]
    width = taps.shape[1]
    kheads, vheads = q.shape[1] // DH, v.shape[1] // DH
    ratio = vheads // kheads
    group = 2 if kheads % 2 == 0 else 1
    shapes = [(q, BF), (k, BF), (v, BF), (beta, F32), (gc, F32), (gr, F32)]
    square = (DH, DH)
    vmem = pl.BlockSpec(memory_space=pltpu.VMEM)
    return pl.pallas_call(
        functools.partial(core_kernel, kheads, ratio, group),
        out_shape=[jax.ShapeDtypeStruct(a.shape, kind) for a, kind in shapes],
        in_specs=[vmem] * 8,
        out_specs=[vmem] * 6,
        scratch_shapes=[
            pltpu.VMEM(q.shape, F32),
            pltpu.VMEM(k.shape, F32),
            pltpu.VMEM(v.shape, F32),
            pltpu.VMEM((size + 16, width), F32),
            pltpu.VMEM((size + 16, width), F32),
            pltpu.VMEM((size + 8, width), F32),
            pltpu.VMEM((16, width), BF),
            pltpu.VMEM((16, width), BF),
            pltpu.VMEM((8, width), F32),
            pltpu.SemaphoreType.DMA((4,)),
            pltpu.VMEM((vheads, size, size), BF),
            pltpu.VMEM((vheads, size, DH), BF),
            pltpu.VMEM((vheads, size, DH), F32),
            pltpu.VMEM((vheads, size, DH), F32),
            pltpu.VMEM((2, vheads) + square, BF),
            pltpu.VMEM((2, vheads) + square, F32),
            pltpu.VMEM((vheads, 8, DH), F32),
            pltpu.VMEM((2, vheads) + square, BF),
            pltpu.VMEM((2, vheads) + square, BF),
            pltpu.SemaphoreType.DMA((2, vheads)),
            pltpu.SemaphoreType.DMA((2, vheads)),
        ],
        compiler_params=pltpu.CompilerParams(
            collective_id=0, has_side_effects=True, vmem_limit_bytes=40 * 1024 * 1024
        ),
    )(q, k, v, taps, beta, gc, gr, grad_core)


def running_sum(log_decay):
    size = log_decay.shape[0]
    row = lax.broadcasted_iota(jnp.int32, (size, size), 0)
    col = lax.broadcasted_iota(jnp.int32, (size, size), 1)
    return jnp.dot(
        jnp.where(row >= col, 1.0, 0.0), log_decay, precision=lax.Precision.HIGHEST,
        preferred_element_type=F32,
    )


def local(
    inputs, query_weight, key_weight, value_weight, beta_weight, alpha_weight,
    query_filter, key_filter, value_filter, decay_log, step_bias, grad_core,
):
    weights = (query_weight, key_weight, value_weight, beta_weight, alpha_weight)
    pair = lax.axis_size("tp") == 2
    side = lax.axis_index("tp")
    if pair:
        other = lax.ppermute(inputs, "tp", [(0, 1), (1, 0)])
        whole = jnp.where(
            side == 0,
            jnp.concatenate([inputs, other], 1),
            jnp.concatenate([other, inputs], 1),
        )
    else:
        whole = lax.all_gather(inputs, "tp", axis=1, tiled=True)
    rounded = lax.optimization_barrier(
        tuple(jnp.dot(whole, w, preferred_element_type=F32).astype(BF) for w in weights)
    )
    taps = jnp.concatenate([query_filter, key_filter, value_filter], 1).astype(F32)

    def front(beta_raw, alpha_raw):
        beta = jax.nn.sigmoid(beta_raw)
        log_decay = -jnp.exp(decay_log) * jax.nn.softplus(alpha_raw + step_bias)
        return beta, running_sum(log_decay)

    (beta, gc), front_vjp = jax.vjp(front, rounded[3].astype(F32), rounded[4].astype(F32))
    dq, dk, dv, dbeta, dgc, dgr = recurrence_grads(
        *rounded[:3], taps, beta, gc, gc.T, grad_core
    )
    grads = front_vjp((dbeta, dgc + dgr.T))
    full = [dq, dk, dv] + [g.astype(BF) for g in grads]

    def contribution(pieces):
        total = 0.0
        for grad_rows, weight in zip(full, pieces):
            total = total + lax.dot_general(
                grad_rows, weight, (((1,), (1,)), ((), ())), preferred_element_type=F32
            )
        return total

    share = inputs.shape[1]
    if pair:
        far = contribution(
            [lax.dynamic_slice_in_dim(w, (1 - side) * share, share, 0) for w in weights]
        ).astype(BF)
        arrived = lax.ppermute(far, "tp", [(0, 1), (1, 0)])
        near = contribution(
            [lax.dynamic_slice_in_dim(w, side * share, share, 0) for w in weights]
        )
        return (near + arrived.astype(F32)).astype(BF)
    return lax.psum_scatter(
        contribution(weights).astype(BF), "tp", scatter_dimension=1, tiled=True
    )


def solution(mesh):
    return jax.shard_map(
        local,
        mesh=mesh,
        in_specs=(
            P("ctx", "tp"),
            P(None, "tp"),
            P(None, "tp"),
            P(None, "tp"),
            P(None, "tp"),
            P(None, "tp"),
            P(None, "tp"),
            P(None, "tp"),
            P(None, "tp"),
            P("tp"),
            P("tp"),
            P("ctx", "tp"),
        ),
        out_specs=P("ctx", "tp"),
        check_vma=False,
    )
```

```python
import functools

import jax
import jax.numpy as jnp
from jax import lax
from jax.experimental import pallas as pl
from jax.experimental.pallas import tpu as pltpu
from jax.sharding import PartitionSpec as P

DH = 128
CONV = 4
EPS = 1e-06
MESH = pl.DeviceIdType.MESH
BF = jnp.bfloat16
F32 = jnp.float32


def mm(left, right, lc, rc):
    return lax.dot_general(
        left.astype(BF), right.astype(BF), (((lc,), (rc,)), ((), ())), preferred_element_type=F32
    )


def nn(left, right):
    return mm(left, right, 1, 0)


def nt(left, right):
    return mm(left, right, 1, 1)


def tn(left, right):
    return mm(left, right, 0, 0)


def rowsum(value):
    return jnp.sum(value, axis=1, keepdims=True)


def colsum(value):
    return jnp.sum(value, axis=0, keepdims=True)


def column(ref, head):
    value = ref[...]
    lanes = lax.broadcasted_iota(jnp.int32, value.shape, 1)
    return rowsum(jnp.where(lanes == head, value, 0.0))


def lane_block(head):
    return pl.ds(pl.multiple_of(head * DH, DH), DH)


def inverses(stricts):
    size = stricts[0].shape[0]
    row = lax.broadcasted_iota(jnp.int32, (size, size), 0)
    col = lax.broadcasted_iota(jnp.int32, (size, size), 1)
    results = [jnp.where(row == col, 1.0, 0.0) - jnp.where((row // 2) == (col // 2), a, 0.0) for a in stricts]
    block = 2
    while block < size:
        within = ((row // (2 * block)) == (col // (2 * block))) & ((row // block) > (col // block))
        parts = [jnp.where(within, a, 0.0) for a in stricts]
        halves = [nn(a, m) for a, m in zip(parts, results)]
        results = [m - nn(m, a) for m, a in zip(results, halves)]
        block *= 2
    return results


def core_kernel(
    kheads, ratio, group,
    pq_ref, pk_ref, pv_ref, taps_ref, beta_ref, gc_ref, gr_ref, do_ref,
    dpq_ref, dpk_ref, dpv_ref, dbeta_ref, dgc_ref, dgr_ref,
    q_ref, k_ref, v_ref, pad_s, run_s, dpad_s, tail_s, tail_land, dtail_land,
    tail_sems, inv_s, w_s, vm_s, y_s, move_s, add_s, end_s, land_s, out_s,
    send_sem, recv_sem,
):
    count, me = lax.axis_size("ctx"), lax.axis_index("ctx")
    vheads = kheads * ratio
    size = pq_ref.shape[0]
    kw, vw = pq_ref.shape[1], pv_ref.shape[1]
    width = 2 * kw + vw
    projected = ((pq_ref, 0, kw), (pk_ref, kw, kw), (pv_ref, 2 * kw, vw))
    row = lax.broadcasted_iota(jnp.int32, (size, size), 0)
    col = lax.broadcasted_iota(jnp.int32, (size, size), 1)
    lower, strictly = row >= col, row > col

    barrier = pltpu.get_barrier_semaphore()

    @pl.when(me > 0)
    def _():
        pl.semaphore_signal(barrier, inc=1, device_id={"ctx": me - 1}, device_id_type=MESH)

    @pl.when(me < count - 1)
    def _():
        pl.semaphore_signal(barrier, inc=1, device_id={"ctx": me + 1}, device_id_type=MESH)

    peers = jnp.minimum(me, 1) + jnp.minimum(count - 1 - me, 1)
    pl.semaphore_wait(barrier, peers)

    def tail_copy():
        return pltpu.make_async_remote_copy(
            src_ref=tail_s, dst_ref=tail_land, send_sem=tail_sems.at[0], recv_sem=tail_sems.at[1],
            device_id={"ctx": me + 1}, device_id_type=MESH,
        )

    def dtail_copy():
        return pltpu.make_async_remote_copy(
            src_ref=dpad_s.at[0:8], dst_ref=dtail_land, send_sem=tail_sems.at[2],
            recv_sem=tail_sems.at[3], device_id={"ctx": me - 1}, device_id_type=MESH,
        )

    for ref, at, wide in projected:
        tail_s[:, at : at + wide] = ref[size - 16 : size, :]

    @pl.when(me < count - 1)
    def _():
        tail_copy().start()

    for ref, at, wide in projected:
        pad_s[16 : 16 + size, at : at + wide] = ref[...].astype(F32)
    run_s[0:8, :] = jnp.zeros((8, width), F32)
    run_s[8 + size : 16 + size, :] = jnp.zeros((8, width), F32)

    @pl.when(me == 0)
    def _():
        tail_land[...] = jnp.zeros(tail_land.shape, tail_land.dtype)

    @pl.when(me == count - 1)
    def _():
        dtail_land[...] = jnp.zeros(dtail_land.shape, dtail_land.dtype)

    @pl.when(me > 0)
    def _():
        tail_copy().wait_recv()

    pad_s[0:16, :] = tail_land[...].astype(F32)

    def convolved(block):
        lanes = lane_block(block)
        taps = taps_ref[:, lanes]
        total = taps[0:1, :] * pad_s[16 - CONV + 1 : 16 - CONV + 1 + size, lanes]
        for tap in range(1, CONV):
            first = 16 - CONV + 1 + tap
            total += taps[tap : tap + 1, :] * pad_s[first : first + size, lanes]
        gate = 1.0 / (1.0 + jnp.exp(-total))
        return total, gate

    def unit(act):
        return lax.rsqrt(rowsum(act * act) + EPS)

    def front_qk(head, carry):
        for ref, first, scale in ((q_ref, 0, DH ** (-0.5)), (k_ref, kheads, 1.0)):
            total, gate = convolved(first + head)
            act = total * gate
            ref[:, lane_block(head)] = act * (unit(act) * scale)
        return carry

    def front_v(head, carry):
        total, gate = convolved(2 * kheads + head)
        v_ref[:, lane_block(head)] = total * gate
        return carry

    lax.fori_loop(0, kheads, front_qk, 0)
    lax.fori_loop(0, vheads, front_v, 0)

    def front_back(block, grad, scale):
        total, gate = convolved(block)
        if scale is not None:
            act = total * gate
            length = unit(act)
            grad = (scale * length) * (grad - act * (length * length * rowsum(act * grad)))
        run_s[8 : 8 + size, lane_block(block)] = grad * (gate * (1.0 + total * (1.0 - gate)))

    def gates(head):
        gc, gr = column(gc_ref, head), gr_ref[pl.ds(head, 1), :]
        decay = jnp.where(lower, jnp.exp(jnp.where(lower, gc - gr, 0.0)), 0.0)
        last = gc[size - 1 : size, :]
        return column(beta_ref, head), decay, jnp.exp(gc), jnp.exp(last - gc), jnp.exp(last)

    def prepare(step, carry):
        kh = [step * group + i for i in range(group)]
        ks = [k_ref[:, lane_block(h)] for h in kh]
        qs = [q_ref[:, lane_block(h)] for h in kh]
        kk = [nt(k, k) for k in ks]
        qk = [nt(q, k) for q, k in zip(qs, ks)]
        heads = [(i, kh[i] * ratio + r) for i in range(group) for r in range(ratio)]
        gate = [gates(h) for _, h in heads]
        stricts = [
            jnp.where(strictly, g[0] * kk[i] * g[1], 0.0) for (i, _), g in zip(heads, gate)
        ]
        invs = inverses(stricts)
        dos = [do_ref[:, lane_block(h)] for _, h in heads]
        ys = [tn(qk[i] * g[1], do) for (i, _), g, do in zip(heads, gate, dos)]
        ws = [nn(m, (g[0] * g[2]) * ks[i]) for (i, _), g, m in zip(heads, gate, invs)]
        vms = [nn(m, g[0] * v_ref[:, lane_block(h)]) for (_, h), g, m in zip(heads, gate, invs)]
        kts = [g[3] * ks[i] for (i, _), g in zip(heads, gate)]
        for n, (i, h) in enumerate(heads):
            inv_s[h] = invs[n].astype(BF)
            w_s[h] = ws[n].astype(BF)
            vm_s[h] = vms[n]
            y_s[h] = ys[n]
            end_s[h] = jnp.broadcast_to(gate[n][4], (8, DH))
            move_s[0, h] = tn(kts[n], ws[n]).astype(BF)
            move_s[1, h] = tn(ws[n], kts[n]).astype(BF)
            add_s[0, h] = tn(kts[n], vms[n])
            add_s[1, h] = tn(gate[n][2] * qs[i], dos[n]) - tn(ws[n], ys[n])
        return carry

    lax.fori_loop(0, kheads // group, prepare, 0)

    @pl.when(me == 0)
    def _():
        land_s[0] = jnp.zeros(land_s.shape[1:], land_s.dtype)

    @pl.when(me == count - 1)
    def _():
        land_s[1] = jnp.zeros(land_s.shape[1:], land_s.dtype)

    late = (2 * me) // count

    def hop(way, head, target):
        return pltpu.make_async_remote_copy(
            src_ref=out_s.at[way, head],
            dst_ref=land_s.at[way, head],
            send_sem=send_sem.at[way, head],
            recv_sem=recv_sem.at[way, head],
            device_id={"ctx": target},
            device_id_type=MESH,
        )

    def advance(way, head):
        before, after = me - 1 + 2 * way, me + 1 - 2 * way

        @pl.when((before >= 0) & (before < count))
        def _():
            hop(way, head, before).wait_recv()

        @pl.when((after >= 0) & (after < count))
        def _():
            state = land_s[way, head]
            out_s[way, head] = (
                end_s[head][0:1, :] * state.astype(F32)
                - nn(move_s[way, head], state)
                + add_s[way, head]
            ).astype(BF)
            hop(way, head, after).start()

    lag = jnp.minimum(vheads, 2 * (1 - 2 * late) * (count - 1 - 2 * me))

    def leading(head, carry):
        advance(late, head)
        return carry

    def mixed(head, carry):
        advance(1 - late, head)
        advance(late, lag + head)
        return carry

    def trailing(head, carry):
        advance(1 - late, head)
        return carry

    lax.fori_loop(0, lag, leading, 0)
    lax.fori_loop(0, vheads - lag, mixed, 0)
    lax.fori_loop(vheads - lag, vheads, trailing, 0)

    dbeta_ref[...] = jnp.zeros(dbeta_ref.shape, F32)
    dgc_ref[...] = jnp.zeros(dgc_ref.shape, F32)
    gate_lanes = lax.broadcasted_iota(jnp.int32, dbeta_ref.shape, 1)
    at_end = lax.broadcasted_iota(jnp.int32, (size, 1), 0) == size - 1

    def back(step, carry):
        kh = [step * group + i for i in range(group)]
        ks = [k_ref[:, lane_block(h)] for h in kh]
        qs = [q_ref[:, lane_block(h)] for h in kh]
        kk = [nt(k, k) for k in ks]
        qk = [nt(q, k) for q, k in zip(qs, ks)]
        heads = [(i, kh[i] * ratio + r) for i in range(group) for r in range(ratio)]
        span = range(len(heads))
        gate = [gates(h) for _, h in heads]
        own_k = [ks[i] for i, _ in heads]
        own_q = [qs[i] for i, _ in heads]
        dos = [do_ref[:, lane_block(h)] for _, h in heads]
        vs = [v_ref[:, lane_block(h)] for _, h in heads]
        starts = [land_s[0, h] for _, h in heads]
        ends = [land_s[1, h] for _, h in heads]
        fresh = [vm_s[h] - nn(w_s[h], starts[n]) for n, (_, h) in enumerate(heads)]
        xs = [nn(own_k[n], starts[n]) for n in span]
        dfresh = [
            y_s[h] + nn(gate[n][3] * own_k[n], ends[n]) for n, (_, h) in enumerate(heads)
        ]
        drs = [tn(inv_s[h], dfresh[n]) for n, (_, h) in enumerate(heads)]
        dps = [nt(dos[n], fresh[n]) for n in span]
        dqs = [nt(dos[n], starts[n]) for n in span]
        dkt = [nt(fresh[n], ends[n]) for n in span]
        das = [jnp.where(strictly, -nt(drs[n], fresh[n]), 0.0) for n in span]
        dxs = [nt((gate[n][0] * gate[n][2]) * drs[n], starts[n]) for n in span]
        dqk = [0.0] * group
        dkk = [0.0] * group
        dq = [0.0] * group
        dk = [0.0] * group
        for n, (i, h) in enumerate(heads):
            beta, decay, gam, tail, end = gate[n]
            k, q = own_k[n], own_q[n]
            dpd = dps[n] * decay
            dad = das[n] * decay
            dad_kk = dad * kk[i]
            dqk[i] += dpd
            dkk[i] += beta * dad
            logs = dpd * qk[i] + beta * dad_kk
            dgam = rowsum(q * dqs[n]) - beta * rowsum(drs[n] * xs[n])
            dtail = rowsum(k * dkt[n]) * tail
            dend = jnp.sum(
                starts[n].astype(F32) * ends[n].astype(F32), axis=(0, 1), keepdims=True
            ) * end
            dbeta = rowsum(drs[n] * (vs[n] - gam * xs[n])) + rowsum(dad_kk)
            dgc = rowsum(logs) + dgam * gam - dtail
            dgc += jnp.where(at_end, colsum(dtail) + dend, 0.0)
            dq[i] += gam * dqs[n]
            dk[i] += tail * dkt[n] - dxs[n]
            front_back(2 * kheads + h, beta * drs[n], None)
            dbeta_ref[...] += jnp.where(gate_lanes == h, dbeta, 0.0)
            dgc_ref[...] += jnp.where(gate_lanes == h, dgc, 0.0)
            dgr_ref[pl.ds(h, 1), :] = -colsum(logs)
        for i in range(group):
            front_back(kh[i], dq[i] + nn(dqk[i], ks[i]), DH ** (-0.5))
            front_back(
                kheads + kh[i],
                dk[i] + tn(dqk[i], qs[i]) + nn(dkk[i], ks[i]) + tn(dkk[i], ks[i]),
                1.0,
            )
        return carry

    lax.fori_loop(0, kheads // group, back, 0)

    def transposed(block, carry):
        lanes = lane_block(block)
        taps = taps_ref[:, lanes]
        total = taps[0:1, :] * run_s[CONV - 1 : CONV + 7 + size, lanes]
        for tap in range(1, CONV):
            first = CONV - 1 - tap
            total += taps[tap : tap + 1, :] * run_s[first : first + 8 + size, lanes]
        dpad_s[:, lanes] = total
        return carry

    lax.fori_loop(0, width // DH, transposed, 0)

    @pl.when(me > 0)
    def _():
        dtail_copy().start()

    cut = size - 16
    for ref, at, wide in ((dpq_ref, 0, kw), (dpk_ref, kw, kw), (dpv_ref, 2 * kw, vw)):
        ref[0:cut, :] = dpad_s[8 : 8 + cut, at : at + wide].astype(BF)

    @pl.when(me < count - 1)
    def _():
        dtail_copy().wait_recv()

    for ref, at, wide in ((dpq_ref, 0, kw), (dpk_ref, kw, kw), (dpv_ref, 2 * kw, vw)):
        ref[cut:size, :] = jnp.concatenate(
            [
                dpad_s[8 + cut : size, at : at + wide],
                dpad_s[size : 8 + size, at : at + wide] + dtail_land[:, at : at + wide],
            ],
            0,
        ).astype(BF)

    @pl.when(me < count - 1)
    def _():
        tail_copy().wait_send()

    @pl.when(me > 0)
    def _():
        dtail_copy().wait_send()

    def drain(head, carry):
        @pl.when(me < count - 1)
        def _():
            hop(0, head, me + 1).wait_send()

        @pl.when(me > 0)
        def _():
            hop(1, head, me - 1).wait_send()

        return carry

    lax.fori_loop(0, vheads, drain, 0)


def recurrence_grads(q, k, v, taps, beta, gc, gr, grad_core):
    size = q.shape[0]
    width = taps.shape[1]
    kheads, vheads = q.shape[1] // DH, v.shape[1] // DH
    ratio = vheads // kheads
    group = 2 if kheads % 2 == 0 else 1
    shapes = [(q, BF), (k, BF), (v, BF), (beta, F32), (gc, F32), (gr, F32)]
    square = (DH, DH)
    vmem = pl.BlockSpec(memory_space=pltpu.VMEM)
    return pl.pallas_call(
        functools.partial(core_kernel, kheads, ratio, group),
        out_shape=[jax.ShapeDtypeStruct(a.shape, kind) for a, kind in shapes],
        in_specs=[vmem] * 8,
        out_specs=[vmem] * 6,
        scratch_shapes=[
            pltpu.VMEM(q.shape, F32),
            pltpu.VMEM(k.shape, F32),
            pltpu.VMEM(v.shape, F32),
            pltpu.VMEM((size + 16, width), F32),
            pltpu.VMEM((size + 16, width), F32),
            pltpu.VMEM((size + 8, width), F32),
            pltpu.VMEM((16, width), BF),
            pltpu.VMEM((16, width), BF),
            pltpu.VMEM((8, width), F32),
            pltpu.SemaphoreType.DMA((4,)),
            pltpu.VMEM((vheads, size, size), BF),
            pltpu.VMEM((vheads, size, DH), BF),
            pltpu.VMEM((vheads, size, DH), F32),
            pltpu.VMEM((vheads, size, DH), F32),
            pltpu.VMEM((2, vheads) + square, BF),
            pltpu.VMEM((2, vheads) + square, F32),
            pltpu.VMEM((vheads, 8, DH), F32),
            pltpu.VMEM((2, vheads) + square, BF),
            pltpu.VMEM((2, vheads) + square, BF),
            pltpu.SemaphoreType.DMA((2, vheads)),
            pltpu.SemaphoreType.DMA((2, vheads)),
        ],
        compiler_params=pltpu.CompilerParams(
            collective_id=0, has_side_effects=True, vmem_limit_bytes=40 * 1024 * 1024
        ),
    )(q, k, v, taps, beta, gc, gr, grad_core)


def running_sum(log_decay):
    size = log_decay.shape[0]
    row = lax.broadcasted_iota(jnp.int32, (size, size), 0)
    col = lax.broadcasted_iota(jnp.int32, (size, size), 1)
    return jnp.dot(
        jnp.where(row >= col, 1.0, 0.0), log_decay, precision=lax.Precision.HIGHEST,
        preferred_element_type=F32,
    )


def local(
    inputs, query_weight, key_weight, value_weight, beta_weight, alpha_weight,
    query_filter, key_filter, value_filter, decay_log, step_bias, grad_core,
):
    weights = (query_weight, key_weight, value_weight, beta_weight, alpha_weight)
    pair = lax.axis_size("tp") == 2
    side = lax.axis_index("tp")
    if pair:
        other = lax.ppermute(inputs, "tp", [(0, 1), (1, 0)])
        whole = jnp.where(
            side == 0,
            jnp.concatenate([inputs, other], 1),
            jnp.concatenate([other, inputs], 1),
        )
    else:
        whole = lax.all_gather(inputs, "tp", axis=1, tiled=True)
    rounded = lax.optimization_barrier(
        tuple(jnp.dot(whole, w, preferred_element_type=F32).astype(BF) for w in weights)
    )
    taps = jnp.concatenate([query_filter, key_filter, value_filter], 1).astype(F32)

    def front(beta_raw, alpha_raw):
        beta = jax.nn.sigmoid(beta_raw)
        log_decay = -jnp.exp(decay_log) * jax.nn.softplus(alpha_raw + step_bias)
        return beta, running_sum(log_decay)

    (beta, gc), front_vjp = jax.vjp(front, rounded[3].astype(F32), rounded[4].astype(F32))
    dq, dk, dv, dbeta, dgc, dgr = recurrence_grads(
        *rounded[:3], taps, beta, gc, gc.T, grad_core
    )
    grads = front_vjp((dbeta, dgc + dgr.T))
    full = [dq, dk, dv] + [g.astype(BF) for g in grads]

    total = 0.0
    for grad_rows, weight in zip(full, weights):
        total = total + lax.dot_general(
            grad_rows, weight, (((1,), (1,)), ((), ())), preferred_element_type=F32
        )
    share = inputs.shape[1]
    if pair:
        far = lax.dynamic_slice_in_dim(total, (1 - side) * share, share, 1).astype(BF)
        arrived = lax.ppermute(far, "tp", [(0, 1), (1, 0)])
        near = lax.dynamic_slice_in_dim(total, side * share, share, 1)
        return (near + arrived.astype(F32)).astype(BF)
    return lax.psum_scatter(
        total.astype(BF), "tp", scatter_dimension=1, tiled=True
    )


def solution(mesh):
    return jax.shard_map(
        local,
        mesh=mesh,
        in_specs=(
            P("ctx", "tp"),
            P(None, "tp"),
            P(None, "tp"),
            P(None, "tp"),
            P(None, "tp"),
            P(None, "tp"),
            P(None, "tp"),
            P(None, "tp"),
            P(None, "tp"),
            P("tp"),
            P("tp"),
            P("ctx", "tp"),
        ),
        out_specs=P("ctx", "tp"),
        check_vma=False,
    )
```

```python
import functools

import jax
import jax.numpy as jnp
from jax import lax
from jax.experimental import pallas as pl
from jax.experimental.pallas import tpu as pltpu
from jax.sharding import PartitionSpec as P

DH = 128
CONV = 4
EPS = 1e-06
MESH = pl.DeviceIdType.MESH
BF = jnp.bfloat16
F32 = jnp.float32


def mm(left, right, lc, rc):
    return lax.dot_general(
        left.astype(BF), right.astype(BF), (((lc,), (rc,)), ((), ())), preferred_element_type=F32
    )


def nn(left, right):
    return mm(left, right, 1, 0)


def nt(left, right):
    return mm(left, right, 1, 1)


def tn(left, right):
    return mm(left, right, 0, 0)


def rowsum(value):
    return jnp.sum(value, axis=1, keepdims=True)


def colsum(value):
    return jnp.sum(value, axis=0, keepdims=True)


def column(ref, head):
    value = ref[...]
    lanes = lax.broadcasted_iota(jnp.int32, value.shape, 1)
    return rowsum(jnp.where(lanes == head, value, 0.0))


def lane_block(head):
    return pl.ds(pl.multiple_of(head * DH, DH), DH)


def inverses(stricts):
    size = stricts[0].shape[0]
    row = lax.broadcasted_iota(jnp.int32, (size, size), 0)
    col = lax.broadcasted_iota(jnp.int32, (size, size), 1)
    results = [jnp.where(row == col, 1.0, 0.0) - jnp.where((row // 2) == (col // 2), a, 0.0) for a in stricts]
    block = 2
    while block < size:
        within = ((row // (2 * block)) == (col // (2 * block))) & ((row // block) > (col // block))
        parts = [jnp.where(within, a, 0.0) for a in stricts]
        halves = [nn(a, m) for a, m in zip(parts, results)]
        results = [m - nn(m, a) for m, a in zip(results, halves)]
        block *= 2
    return results


def core_kernel(
    kheads, ratio, group,
    pq_ref, pk_ref, pv_ref, taps_ref, beta_ref, gc_ref, gr_ref, do_ref,
    dpq_ref, dpk_ref, dpv_ref, dbeta_ref, dgc_ref, dgr_ref,
    q_ref, k_ref, v_ref, pad_s, run_s, dpad_s, tail_s, tail_land, dtail_land,
    tail_sems, inv_s, w_s, vm_s, y_s, move_s, add_s, end_s, land_s, out_s,
    send_sem, recv_sem,
):
    count, me = lax.axis_size("ctx"), lax.axis_index("ctx")
    vheads = kheads * ratio
    size = pq_ref.shape[0]
    kw, vw = pq_ref.shape[1], pv_ref.shape[1]
    width = 2 * kw + vw
    projected = ((pq_ref, 0, kw), (pk_ref, kw, kw), (pv_ref, 2 * kw, vw))
    row = lax.broadcasted_iota(jnp.int32, (size, size), 0)
    col = lax.broadcasted_iota(jnp.int32, (size, size), 1)
    lower, strictly = row >= col, row > col

    barrier = pltpu.get_barrier_semaphore()

    @pl.when(me > 0)
    def _():
        pl.semaphore_signal(barrier, inc=1, device_id={"ctx": me - 1}, device_id_type=MESH)

    @pl.when(me < count - 1)
    def _():
        pl.semaphore_signal(barrier, inc=1, device_id={"ctx": me + 1}, device_id_type=MESH)

    peers = jnp.minimum(me, 1) + jnp.minimum(count - 1 - me, 1)
    pl.semaphore_wait(barrier, peers)

    def tail_copy():
        return pltpu.make_async_remote_copy(
            src_ref=tail_s, dst_ref=tail_land, send_sem=tail_sems.at[0], recv_sem=tail_sems.at[1],
            device_id={"ctx": me + 1}, device_id_type=MESH,
        )

    def dtail_copy():
        return pltpu.make_async_remote_copy(
            src_ref=dpad_s.at[0:8], dst_ref=dtail_land, send_sem=tail_sems.at[2],
            recv_sem=tail_sems.at[3], device_id={"ctx": me - 1}, device_id_type=MESH,
        )

    for ref, at, wide in projected:
        tail_s[:, at : at + wide] = ref[size - 16 : size, :]

    @pl.when(me < count - 1)
    def _():
        tail_copy().start()

    for ref, at, wide in projected:
        pad_s[16 : 16 + size, at : at + wide] = ref[...].astype(F32)
    run_s[0:8, :] = jnp.zeros((8, width), F32)
    run_s[8 + size : 16 + size, :] = jnp.zeros((8, width), F32)

    @pl.when(me == 0)
    def _():
        tail_land[...] = jnp.zeros(tail_land.shape, tail_land.dtype)

    @pl.when(me == count - 1)
    def _():
        dtail_land[...] = jnp.zeros(dtail_land.shape, dtail_land.dtype)

    @pl.when(me > 0)
    def _():
        tail_copy().wait_recv()

    pad_s[0:16, :] = tail_land[...].astype(F32)

    def convolved(block):
        lanes = lane_block(block)
        taps = taps_ref[:, lanes]
        total = taps[0:1, :] * pad_s[16 - CONV + 1 : 16 - CONV + 1 + size, lanes]
        for tap in range(1, CONV):
            first = 16 - CONV + 1 + tap
            total += taps[tap : tap + 1, :] * pad_s[first : first + size, lanes]
        gate = 1.0 / (1.0 + jnp.exp(-total))
        return total, gate

    def unit(act):
        return lax.rsqrt(rowsum(act * act) + EPS)

    def front_qk(head, carry):
        for ref, first, scale in ((q_ref, 0, DH ** (-0.5)), (k_ref, kheads, 1.0)):
            total, gate = convolved(first + head)
            act = total * gate
            ref[:, lane_block(head)] = act * (unit(act) * scale)
        return carry

    def front_v(head, carry):
        total, gate = convolved(2 * kheads + head)
        v_ref[:, lane_block(head)] = total * gate
        return carry

    lax.fori_loop(0, kheads, front_qk, 0)
    lax.fori_loop(0, vheads, front_v, 0)

    def front_back(block, grad, scale):
        total, gate = convolved(block)
        if scale is not None:
            act = total * gate
            length = unit(act)
            grad = (scale * length) * (grad - act * (length * length * rowsum(act * grad)))
        run_s[8 : 8 + size, lane_block(block)] = grad * (gate * (1.0 + total * (1.0 - gate)))

    def gates(head):
        gc, gr = column(gc_ref, head), gr_ref[pl.ds(head, 1), :]
        decay = jnp.where(lower, jnp.exp(jnp.where(lower, gc - gr, 0.0)), 0.0)
        last = gc[size - 1 : size, :]
        return column(beta_ref, head), decay, jnp.exp(gc), jnp.exp(last - gc), jnp.exp(last)

    def prepare(step, carry):
        kh = [step * group + i for i in range(group)]
        ks = [k_ref[:, lane_block(h)] for h in kh]
        qs = [q_ref[:, lane_block(h)] for h in kh]
        kk = [nt(k, k) for k in ks]
        qk = [nt(q, k) for q, k in zip(qs, ks)]
        heads = [(i, kh[i] * ratio + r) for i in range(group) for r in range(ratio)]
        gate = [gates(h) for _, h in heads]
        stricts = [
            jnp.where(strictly, g[0] * kk[i] * g[1], 0.0) for (i, _), g in zip(heads, gate)
        ]
        invs = inverses(stricts)
        dos = [do_ref[:, lane_block(h)] for _, h in heads]
        ys = [tn(qk[i] * g[1], do) for (i, _), g, do in zip(heads, gate, dos)]
        ws = [nn(m, (g[0] * g[2]) * ks[i]) for (i, _), g, m in zip(heads, gate, invs)]
        vms = [nn(m, g[0] * v_ref[:, lane_block(h)]) for (_, h), g, m in zip(heads, gate, invs)]
        kts = [g[3] * ks[i] for (i, _), g in zip(heads, gate)]
        for n, (i, h) in enumerate(heads):
            inv_s[h] = invs[n].astype(BF)
            w_s[h] = ws[n].astype(BF)
            vm_s[h] = vms[n]
            y_s[h] = ys[n]
            end_s[h] = jnp.broadcast_to(gate[n][4], (8, DH))
            move_s[0, h] = tn(kts[n], ws[n]).astype(BF)
            move_s[1, h] = tn(ws[n], kts[n]).astype(BF)
            add_s[0, h] = tn(kts[n], vms[n])
            add_s[1, h] = tn(gate[n][2] * qs[i], dos[n]) - tn(ws[n], ys[n])
        return carry

    lax.fori_loop(0, kheads // group, prepare, 0)

    @pl.when(me == 0)
    def _():
        land_s[0] = jnp.zeros(land_s.shape[1:], land_s.dtype)

    @pl.when(me == count - 1)
    def _():
        land_s[1] = jnp.zeros(land_s.shape[1:], land_s.dtype)

    late = (2 * me) // count

    def hop(way, head, target):
        return pltpu.make_async_remote_copy(
            src_ref=out_s.at[way, head],
            dst_ref=land_s.at[way, head],
            send_sem=send_sem.at[way, head],
            recv_sem=recv_sem.at[way, head],
            device_id={"ctx": target},
            device_id_type=MESH,
        )

    def chain(step, carry):
        turn, head = step // vheads, step % vheads
        way = turn + late - 2 * turn * late
        before, after = me - 1 + 2 * way, me + 1 - 2 * way

        @pl.when((before >= 0) & (before < count) & ((turn == 0) | ((after >= 0) & (after < count))))
        def _():
            hop(way, head, before).wait_recv()

        @pl.when((after >= 0) & (after < count))
        def _():
            state = land_s[way, head]
            out_s[way, head] = (
                end_s[head][0:1, :] * state.astype(F32)
                - nn(move_s[way, head], state)
                + add_s[way, head]
            ).astype(BF)
            hop(way, head, after).start()

        return carry

    lax.fori_loop(0, 2 * vheads, chain, 0)

    dbeta_ref[...] = jnp.zeros(dbeta_ref.shape, F32)
    dgc_ref[...] = jnp.zeros(dgc_ref.shape, F32)
    gate_lanes = lax.broadcasted_iota(jnp.int32, dbeta_ref.shape, 1)
    at_end = lax.broadcasted_iota(jnp.int32, (size, 1), 0) == size - 1

    def back(step, carry):
        kh = [step * group + i for i in range(group)]
        ks = [k_ref[:, lane_block(h)] for h in kh]
        qs = [q_ref[:, lane_block(h)] for h in kh]
        kk = [nt(k, k) for k in ks]
        qk = [nt(q, k) for q, k in zip(qs, ks)]
        heads = [(i, kh[i] * ratio + r) for i in range(group) for r in range(ratio)]
        span = range(len(heads))

        @pl.when(me == 0)
        def _():
            for _, h in heads:
                hop(1, h, me + 1).wait_recv()

        @pl.when(me == count - 1)
        def _():
            for _, h in heads:
                hop(0, h, me - 1).wait_recv()

        gate = [gates(h) for _, h in heads]
        own_k = [ks[i] for i, _ in heads]
        own_q = [qs[i] for i, _ in heads]
        dos = [do_ref[:, lane_block(h)] for _, h in heads]
        vs = [v_ref[:, lane_block(h)] for _, h in heads]
        starts = [land_s[0, h] for _, h in heads]
        ends = [land_s[1, h] for _, h in heads]
        fresh = [vm_s[h] - nn(w_s[h], starts[n]) for n, (_, h) in enumerate(heads)]
        xs = [nn(own_k[n], starts[n]) for n in span]
        dfresh = [
            y_s[h] + nn(gate[n][3] * own_k[n], ends[n]) for n, (_, h) in enumerate(heads)
        ]
        drs = [tn(inv_s[h], dfresh[n]) for n, (_, h) in enumerate(heads)]
        dps = [nt(dos[n], fresh[n]) for n in span]
        dqs = [nt(dos[n], starts[n]) for n in span]
        dkt = [nt(fresh[n], ends[n]) for n in span]
        das = [jnp.where(strictly, -nt(drs[n], fresh[n]), 0.0) for n in span]
        dxs = [nt((gate[n][0] * gate[n][2]) * drs[n], starts[n]) for n in span]
        dqk = [0.0] * group
        dkk = [0.0] * group
        dq = [0.0] * group
        dk = [0.0] * group
        for n, (i, h) in enumerate(heads):
            beta, decay, gam, tail, end = gate[n]
            k, q = own_k[n], own_q[n]
            dpd = dps[n] * decay
            dad = das[n] * decay
            dad_kk = dad * kk[i]
            dqk[i] += dpd
            dkk[i] += beta * dad
            logs = dpd * qk[i] + beta * dad_kk
            dgam = rowsum(q * dqs[n]) - beta * rowsum(drs[n] * xs[n])
            dtail = rowsum(k * dkt[n]) * tail
            dend = jnp.sum(
                starts[n].astype(F32) * ends[n].astype(F32), axis=(0, 1), keepdims=True
            ) * end
            dbeta = rowsum(drs[n] * (vs[n] - gam * xs[n])) + rowsum(dad_kk)
            dgc = rowsum(logs) + dgam * gam - dtail
            dgc += jnp.where(at_end, colsum(dtail) + dend, 0.0)
            dq[i] += gam * dqs[n]
            dk[i] += tail * dkt[n] - dxs[n]
            front_back(2 * kheads + h, beta * drs[n], None)
            dbeta_ref[...] += jnp.where(gate_lanes == h, dbeta, 0.0)
            dgc_ref[...] += jnp.where(gate_lanes == h, dgc, 0.0)
            dgr_ref[pl.ds(h, 1), :] = -colsum(logs)
        for i in range(group):
            front_back(kh[i], dq[i] + nn(dqk[i], ks[i]), DH ** (-0.5))
            front_back(
                kheads + kh[i],
                dk[i] + tn(dqk[i], qs[i]) + nn(dkk[i], ks[i]) + tn(dkk[i], ks[i]),
                1.0,
            )
        return carry

    lax.fori_loop(0, kheads // group, back, 0)

    def transposed(block, carry):
        lanes = lane_block(block)
        taps = taps_ref[:, lanes]
        total = taps[0:1, :] * run_s[CONV - 1 : CONV + 7 + size, lanes]
        for tap in range(1, CONV):
            first = CONV - 1 - tap
            total += taps[tap : tap + 1, :] * run_s[first : first + 8 + size, lanes]
        dpad_s[:, lanes] = total
        return carry

    lax.fori_loop(0, width // DH, transposed, 0)

    @pl.when(me > 0)
    def _():
        dtail_copy().start()

    cut = size - 16
    for ref, at, wide in ((dpq_ref, 0, kw), (dpk_ref, kw, kw), (dpv_ref, 2 * kw, vw)):
        ref[0:cut, :] = dpad_s[8 : 8 + cut, at : at + wide].astype(BF)

    @pl.when(me < count - 1)
    def _():
        dtail_copy().wait_recv()

    for ref, at, wide in ((dpq_ref, 0, kw), (dpk_ref, kw, kw), (dpv_ref, 2 * kw, vw)):
        ref[cut:size, :] = jnp.concatenate(
            [
                dpad_s[8 + cut : size, at : at + wide],
                dpad_s[size : 8 + size, at : at + wide] + dtail_land[:, at : at + wide],
            ],
            0,
        ).astype(BF)

    @pl.when(me < count - 1)
    def _():
        tail_copy().wait_send()

    @pl.when(me > 0)
    def _():
        dtail_copy().wait_send()

    def drain(head, carry):
        @pl.when(me < count - 1)
        def _():
            hop(0, head, me + 1).wait_send()

        @pl.when(me > 0)
        def _():
            hop(1, head, me - 1).wait_send()

        return carry

    lax.fori_loop(0, vheads, drain, 0)


def recurrence_grads(q, k, v, taps, beta, gc, gr, grad_core):
    size = q.shape[0]
    width = taps.shape[1]
    kheads, vheads = q.shape[1] // DH, v.shape[1] // DH
    ratio = vheads // kheads
    group = 2 if kheads % 2 == 0 else 1
    shapes = [(q, BF), (k, BF), (v, BF), (beta, F32), (gc, F32), (gr, F32)]
    square = (DH, DH)
    vmem = pl.BlockSpec(memory_space=pltpu.VMEM)
    return pl.pallas_call(
        functools.partial(core_kernel, kheads, ratio, group),
        out_shape=[jax.ShapeDtypeStruct(a.shape, kind) for a, kind in shapes],
        in_specs=[vmem] * 8,
        out_specs=[vmem] * 6,
        scratch_shapes=[
            pltpu.VMEM(q.shape, F32),
            pltpu.VMEM(k.shape, F32),
            pltpu.VMEM(v.shape, F32),
            pltpu.VMEM((size + 16, width), F32),
            pltpu.VMEM((size + 16, width), F32),
            pltpu.VMEM((size + 8, width), F32),
            pltpu.VMEM((16, width), BF),
            pltpu.VMEM((16, width), BF),
            pltpu.VMEM((8, width), F32),
            pltpu.SemaphoreType.DMA((4,)),
            pltpu.VMEM((vheads, size, size), BF),
            pltpu.VMEM((vheads, size, DH), BF),
            pltpu.VMEM((vheads, size, DH), F32),
            pltpu.VMEM((vheads, size, DH), F32),
            pltpu.VMEM((2, vheads) + square, BF),
            pltpu.VMEM((2, vheads) + square, F32),
            pltpu.VMEM((vheads, 8, DH), F32),
            pltpu.VMEM((2, vheads) + square, BF),
            pltpu.VMEM((2, vheads) + square, BF),
            pltpu.SemaphoreType.DMA((2, vheads)),
            pltpu.SemaphoreType.DMA((2, vheads)),
        ],
        compiler_params=pltpu.CompilerParams(
            collective_id=0, has_side_effects=True, vmem_limit_bytes=40 * 1024 * 1024
        ),
    )(q, k, v, taps, beta, gc, gr, grad_core)


def running_sum(log_decay):
    size = log_decay.shape[0]
    row = lax.broadcasted_iota(jnp.int32, (size, size), 0)
    col = lax.broadcasted_iota(jnp.int32, (size, size), 1)
    return jnp.dot(
        jnp.where(row >= col, 1.0, 0.0), log_decay, precision=lax.Precision.HIGHEST,
        preferred_element_type=F32,
    )


def local(
    inputs, query_weight, key_weight, value_weight, beta_weight, alpha_weight,
    query_filter, key_filter, value_filter, decay_log, step_bias, grad_core,
):
    weights = (query_weight, key_weight, value_weight, beta_weight, alpha_weight)
    pair = lax.axis_size("tp") == 2
    side = lax.axis_index("tp")
    if pair:
        other = lax.ppermute(inputs, "tp", [(0, 1), (1, 0)])
        whole = jnp.where(
            side == 0,
            jnp.concatenate([inputs, other], 1),
            jnp.concatenate([other, inputs], 1),
        )
    else:
        whole = lax.all_gather(inputs, "tp", axis=1, tiled=True)
    rounded = lax.optimization_barrier(
        tuple(jnp.dot(whole, w, preferred_element_type=F32).astype(BF) for w in weights)
    )
    taps = jnp.concatenate([query_filter, key_filter, value_filter], 1).astype(F32)

    def front(beta_raw, alpha_raw):
        beta = jax.nn.sigmoid(beta_raw)
        log_decay = -jnp.exp(decay_log) * jax.nn.softplus(alpha_raw + step_bias)
        return beta, running_sum(log_decay)

    (beta, gc), front_vjp = jax.vjp(front, rounded[3].astype(F32), rounded[4].astype(F32))
    dq, dk, dv, dbeta, dgc, dgr = recurrence_grads(
        *rounded[:3], taps, beta, gc, gc.T, grad_core
    )
    grads = front_vjp((dbeta, dgc + dgr.T))
    full = [dq, dk, dv] + [g.astype(BF) for g in grads]

    total = 0.0
    for grad_rows, weight in zip(full, weights):
        total = total + lax.dot_general(
            grad_rows, weight, (((1,), (1,)), ((), ())), preferred_element_type=F32
        )
    share = inputs.shape[1]
    if pair:
        far = lax.dynamic_slice_in_dim(total, (1 - side) * share, share, 1).astype(BF)
        arrived = lax.ppermute(far, "tp", [(0, 1), (1, 0)])
        near = lax.dynamic_slice_in_dim(total, side * share, share, 1)
        return (near + arrived.astype(F32)).astype(BF)
    return lax.psum_scatter(
        total.astype(BF), "tp", scatter_dimension=1, tiled=True
    )


def solution(mesh):
    return jax.shard_map(
        local,
        mesh=mesh,
        in_specs=(
            P("ctx", "tp"),
            P(None, "tp"),
            P(None, "tp"),
            P(None, "tp"),
            P(None, "tp"),
            P(None, "tp"),
            P(None, "tp"),
            P(None, "tp"),
            P(None, "tp"),
            P("tp"),
            P("tp"),
            P("ctx", "tp"),
        ),
        out_specs=P("ctx", "tp"),
        check_vma=False,
    )
```

```python
import functools

import jax
import jax.numpy as jnp
from jax import lax
from jax.experimental import pallas as pl
from jax.experimental.pallas import tpu as pltpu
from jax.sharding import PartitionSpec as P

DH = 128
CONV = 4
EPS = 1e-06
MESH = pl.DeviceIdType.MESH
BF = jnp.bfloat16
F32 = jnp.float32


def mm(left, right, lc, rc):
    return lax.dot_general(
        left.astype(BF), right.astype(BF), (((lc,), (rc,)), ((), ())), preferred_element_type=F32
    )


def nn(left, right):
    return mm(left, right, 1, 0)


def nt(left, right):
    return mm(left, right, 1, 1)


def tn(left, right):
    return mm(left, right, 0, 0)


def rowsum(value):
    return jnp.sum(value, axis=1, keepdims=True)


def colsum(value):
    return jnp.sum(value, axis=0, keepdims=True)


def column(ref, head):
    value = ref[...]
    lanes = lax.broadcasted_iota(jnp.int32, value.shape, 1)
    return rowsum(jnp.where(lanes == head, value, 0.0))


def lane_block(head):
    return pl.ds(pl.multiple_of(head * DH, DH), DH)


def inverses(stricts):
    size = stricts[0].shape[0]
    row = lax.broadcasted_iota(jnp.int32, (size, size), 0)
    col = lax.broadcasted_iota(jnp.int32, (size, size), 1)
    results = [jnp.where(row == col, 1.0, 0.0) - jnp.where((row // 2) == (col // 2), a, 0.0) for a in stricts]
    block = 2
    while block < size:
        within = ((row // (2 * block)) == (col // (2 * block))) & ((row // block) > (col // block))
        parts = [jnp.where(within, a, 0.0) for a in stricts]
        halves = [nn(a, m) for a, m in zip(parts, results)]
        results = [m - nn(m, a) for m, a in zip(results, halves)]
        block *= 2
    return results


def core_kernel(
    kheads, ratio, group,
    pq_ref, pk_ref, pv_ref, taps_ref, beta_ref, gc_ref, gr_ref, do_ref,
    dpq_ref, dpk_ref, dpv_ref, dbeta_ref, dgc_ref, dgr_ref,
    q_ref, k_ref, v_ref, pad_s, run_s, dpad_s, tail_s, tail_land, dtail_land,
    tail_sems, inv_s, w_s, vm_s, y_s, move_s, add_s, end_s, land_s, out_s,
    send_sem, recv_sem,
):
    count, me = lax.axis_size("ctx"), lax.axis_index("ctx")
    vheads = kheads * ratio
    size = pq_ref.shape[0]
    kw, vw = pq_ref.shape[1], pv_ref.shape[1]
    width = 2 * kw + vw
    projected = ((pq_ref, 0, kw), (pk_ref, kw, kw), (pv_ref, 2 * kw, vw))
    row = lax.broadcasted_iota(jnp.int32, (size, size), 0)
    col = lax.broadcasted_iota(jnp.int32, (size, size), 1)
    lower, strictly = row >= col, row > col

    barrier = pltpu.get_barrier_semaphore()

    @pl.when(me > 0)
    def _():
        pl.semaphore_signal(barrier, inc=1, device_id={"ctx": me - 1}, device_id_type=MESH)

    @pl.when(me < count - 1)
    def _():
        pl.semaphore_signal(barrier, inc=1, device_id={"ctx": me + 1}, device_id_type=MESH)

    peers = jnp.minimum(me, 1) + jnp.minimum(count - 1 - me, 1)
    pl.semaphore_wait(barrier, peers)

    def tail_copy():
        return pltpu.make_async_remote_copy(
            src_ref=tail_s, dst_ref=tail_land, send_sem=tail_sems.at[0], recv_sem=tail_sems.at[1],
            device_id={"ctx": me + 1}, device_id_type=MESH,
        )

    def dtail_copy():
        return pltpu.make_async_remote_copy(
            src_ref=dpad_s.at[0:8], dst_ref=dtail_land, send_sem=tail_sems.at[2],
            recv_sem=tail_sems.at[3], device_id={"ctx": me - 1}, device_id_type=MESH,
        )

    for ref, at, wide in projected:
        tail_s[:, at : at + wide] = ref[size - 16 : size, :]

    @pl.when(me < count - 1)
    def _():
        tail_copy().start()

    for ref, at, wide in projected:
        pad_s[16 : 16 + size, at : at + wide] = ref[...].astype(F32)
    run_s[0:8, :] = jnp.zeros((8, width), F32)
    run_s[8 + size : 16 + size, :] = jnp.zeros((8, width), F32)

    @pl.when(me == 0)
    def _():
        tail_land[...] = jnp.zeros(tail_land.shape, tail_land.dtype)

    @pl.when(me == count - 1)
    def _():
        dtail_land[...] = jnp.zeros(dtail_land.shape, dtail_land.dtype)

    @pl.when(me > 0)
    def _():
        tail_copy().wait_recv()

    pad_s[0:16, :] = tail_land[...].astype(F32)

    def convolved(block):
        lanes = lane_block(block)
        taps = taps_ref[:, lanes]
        total = taps[0:1, :] * pad_s[16 - CONV + 1 : 16 - CONV + 1 + size, lanes]
        for tap in range(1, CONV):
            first = 16 - CONV + 1 + tap
            total += taps[tap : tap + 1, :] * pad_s[first : first + size, lanes]
        gate = 1.0 / (1.0 + jnp.exp(-total))
        return total, gate

    def unit(act):
        return lax.rsqrt(rowsum(act * act) + EPS)

    def front_qk(head, carry):
        for ref, first, scale in ((q_ref, 0, DH ** (-0.5)), (k_ref, kheads, 1.0)):
            total, gate = convolved(first + head)
            act = total * gate
            ref[:, lane_block(head)] = act * (unit(act) * scale)
        return carry

    def front_v(head, carry):
        total, gate = convolved(2 * kheads + head)
        v_ref[:, lane_block(head)] = total * gate
        return carry

    lax.fori_loop(0, kheads, front_qk, 0, unroll=True)
    lax.fori_loop(0, vheads, front_v, 0, unroll=True)

    def front_back(block, grad, scale):
        total, gate = convolved(block)
        if scale is not None:
            act = total * gate
            length = unit(act)
            grad = (scale * length) * (grad - act * (length * length * rowsum(act * grad)))
        run_s[8 : 8 + size, lane_block(block)] = grad * (gate * (1.0 + total * (1.0 - gate)))

    def gates(head):
        gc, gr = column(gc_ref, head), gr_ref[pl.ds(head, 1), :]
        decay = jnp.where(lower, jnp.exp(jnp.where(lower, gc - gr, 0.0)), 0.0)
        last = gc[size - 1 : size, :]
        return column(beta_ref, head), decay, jnp.exp(gc), jnp.exp(last - gc), jnp.exp(last)

    def prepare(step, carry):
        kh = [step * group + i for i in range(group)]
        ks = [k_ref[:, lane_block(h)] for h in kh]
        qs = [q_ref[:, lane_block(h)] for h in kh]
        kk = [nt(k, k) for k in ks]
        qk = [nt(q, k) for q, k in zip(qs, ks)]
        heads = [(i, kh[i] * ratio + r) for i in range(group) for r in range(ratio)]
        gate = [gates(h) for _, h in heads]
        stricts = [
            jnp.where(strictly, g[0] * kk[i] * g[1], 0.0) for (i, _), g in zip(heads, gate)
        ]
        invs = inverses(stricts)
        dos = [do_ref[:, lane_block(h)] for _, h in heads]
        ys = [tn(qk[i] * g[1], do) for (i, _), g, do in zip(heads, gate, dos)]
        ws = [nn(m, (g[0] * g[2]) * ks[i]) for (i, _), g, m in zip(heads, gate, invs)]
        vms = [nn(m, g[0] * v_ref[:, lane_block(h)]) for (_, h), g, m in zip(heads, gate, invs)]
        kts = [g[3] * ks[i] for (i, _), g in zip(heads, gate)]
        for n, (i, h) in enumerate(heads):
            inv_s[h] = invs[n].astype(BF)
            w_s[h] = ws[n].astype(BF)
            vm_s[h] = vms[n]
            y_s[h] = ys[n]
            end_s[h] = jnp.broadcast_to(gate[n][4], (8, DH))
            move_s[0, h] = tn(kts[n], ws[n]).astype(BF)
            move_s[1, h] = tn(ws[n], kts[n]).astype(BF)
            add_s[0, h] = tn(kts[n], vms[n])
            add_s[1, h] = tn(gate[n][2] * qs[i], dos[n]) - tn(ws[n], ys[n])
        return carry

    lax.fori_loop(0, kheads // group, prepare, 0)

    @pl.when(me == 0)
    def _():
        land_s[0] = jnp.zeros(land_s.shape[1:], land_s.dtype)

    @pl.when(me == count - 1)
    def _():
        land_s[1] = jnp.zeros(land_s.shape[1:], land_s.dtype)

    late = (2 * me) // count

    def hop(way, head, target):
        return pltpu.make_async_remote_copy(
            src_ref=out_s.at[way, head],
            dst_ref=land_s.at[way, head],
            send_sem=send_sem.at[way, head],
            recv_sem=recv_sem.at[way, head],
            device_id={"ctx": target},
            device_id_type=MESH,
        )

    def chain(step, carry):
        turn, head = step // vheads, step % vheads
        way = turn + late - 2 * turn * late
        before, after = me - 1 + 2 * way, me + 1 - 2 * way

        @pl.when((before >= 0) & (before < count) & ((turn == 0) | ((after >= 0) & (after < count))))
        def _():
            hop(way, head, before).wait_recv()

        @pl.when((after >= 0) & (after < count))
        def _():
            state = land_s[way, head]
            out_s[way, head] = (
                end_s[head][0:1, :] * state.astype(F32)
                - nn(move_s[way, head], state)
                + add_s[way, head]
            ).astype(BF)
            hop(way, head, after).start()

        return carry

    lax.fori_loop(0, 2 * vheads, chain, 0)

    dbeta_ref[...] = jnp.zeros(dbeta_ref.shape, F32)
    dgc_ref[...] = jnp.zeros(dgc_ref.shape, F32)
    gate_lanes = lax.broadcasted_iota(jnp.int32, dbeta_ref.shape, 1)
    at_end = lax.broadcasted_iota(jnp.int32, (size, 1), 0) == size - 1

    def back(step, carry):
        kh = [step * group + i for i in range(group)]
        ks = [k_ref[:, lane_block(h)] for h in kh]
        qs = [q_ref[:, lane_block(h)] for h in kh]
        kk = [nt(k, k) for k in ks]
        qk = [nt(q, k) for q, k in zip(qs, ks)]
        heads = [(i, kh[i] * ratio + r) for i in range(group) for r in range(ratio)]
        span = range(len(heads))

        @pl.when(me == 0)
        def _():
            for _, h in heads:
                hop(1, h, me + 1).wait_recv()

        @pl.when(me == count - 1)
        def _():
            for _, h in heads:
                hop(0, h, me - 1).wait_recv()

        gate = [gates(h) for _, h in heads]
        own_k = [ks[i] for i, _ in heads]
        own_q = [qs[i] for i, _ in heads]
        dos = [do_ref[:, lane_block(h)] for _, h in heads]
        vs = [v_ref[:, lane_block(h)] for _, h in heads]
        starts = [land_s[0, h] for _, h in heads]
        ends = [land_s[1, h] for _, h in heads]
        fresh = [vm_s[h] - nn(w_s[h], starts[n]) for n, (_, h) in enumerate(heads)]
        xs = [nn(own_k[n], starts[n]) for n in span]
        dfresh = [
            y_s[h] + nn(gate[n][3] * own_k[n], ends[n]) for n, (_, h) in enumerate(heads)
        ]
        drs = [tn(inv_s[h], dfresh[n]) for n, (_, h) in enumerate(heads)]
        dps = [nt(dos[n], fresh[n]) for n in span]
        dqs = [nt(dos[n], starts[n]) for n in span]
        dkt = [nt(fresh[n], ends[n]) for n in span]
        das = [jnp.where(strictly, -nt(drs[n], fresh[n]), 0.0) for n in span]
        dxs = [nt((gate[n][0] * gate[n][2]) * drs[n], starts[n]) for n in span]
        dqk = [0.0] * group
        dkk = [0.0] * group
        dq = [0.0] * group
        dk = [0.0] * group
        for n, (i, h) in enumerate(heads):
            beta, decay, gam, tail, end = gate[n]
            k, q = own_k[n], own_q[n]
            dpd = dps[n] * decay
            dad = das[n] * decay
            dad_kk = dad * kk[i]
            dqk[i] += dpd
            dkk[i] += beta * dad
            logs = dpd * qk[i] + beta * dad_kk
            dgam = rowsum(q * dqs[n]) - beta * rowsum(drs[n] * xs[n])
            dtail = rowsum(k * dkt[n]) * tail
            dend = jnp.sum(
                starts[n].astype(F32) * ends[n].astype(F32), axis=(0, 1), keepdims=True
            ) * end
            dbeta = rowsum(drs[n] * (vs[n] - gam * xs[n])) + rowsum(dad_kk)
            dgc = rowsum(logs) + dgam * gam - dtail
            dgc += jnp.where(at_end, colsum(dtail) + dend, 0.0)
            dq[i] += gam * dqs[n]
            dk[i] += tail * dkt[n] - dxs[n]
            front_back(2 * kheads + h, beta * drs[n], None)
            dbeta_ref[...] += jnp.where(gate_lanes == h, dbeta, 0.0)
            dgc_ref[...] += jnp.where(gate_lanes == h, dgc, 0.0)
            dgr_ref[pl.ds(h, 1), :] = -colsum(logs)
        for i in range(group):
            front_back(kh[i], dq[i] + nn(dqk[i], ks[i]), DH ** (-0.5))
            front_back(
                kheads + kh[i],
                dk[i] + tn(dqk[i], qs[i]) + nn(dkk[i], ks[i]) + tn(dkk[i], ks[i]),
                1.0,
            )
        return carry

    lax.fori_loop(0, kheads // group, back, 0)

    def transposed(block, carry):
        lanes = lane_block(block)
        taps = taps_ref[:, lanes]
        total = taps[0:1, :] * run_s[CONV - 1 : CONV + 7 + size, lanes]
        for tap in range(1, CONV):
            first = CONV - 1 - tap
            total += taps[tap : tap + 1, :] * run_s[first : first + 8 + size, lanes]
        dpad_s[:, lanes] = total
        return carry

    lax.fori_loop(0, width // DH, transposed, 0, unroll=True)

    @pl.when(me > 0)
    def _():
        dtail_copy().start()

    cut = size - 16
    for ref, at, wide in ((dpq_ref, 0, kw), (dpk_ref, kw, kw), (dpv_ref, 2 * kw, vw)):
        ref[0:cut, :] = dpad_s[8 : 8 + cut, at : at + wide].astype(BF)

    @pl.when(me < count - 1)
    def _():
        dtail_copy().wait_recv()

    for ref, at, wide in ((dpq_ref, 0, kw), (dpk_ref, kw, kw), (dpv_ref, 2 * kw, vw)):
        ref[cut:size, :] = jnp.concatenate(
            [
                dpad_s[8 + cut : size, at : at + wide],
                dpad_s[size : 8 + size, at : at + wide] + dtail_land[:, at : at + wide],
            ],
            0,
        ).astype(BF)

    @pl.when(me < count - 1)
    def _():
        tail_copy().wait_send()

    @pl.when(me > 0)
    def _():
        dtail_copy().wait_send()

    def drain(head, carry):
        @pl.when(me < count - 1)
        def _():
            hop(0, head, me + 1).wait_send()

        @pl.when(me > 0)
        def _():
            hop(1, head, me - 1).wait_send()

        return carry

    lax.fori_loop(0, vheads, drain, 0)


def recurrence_grads(q, k, v, taps, beta, gc, gr, grad_core):
    size = q.shape[0]
    width = taps.shape[1]
    kheads, vheads = q.shape[1] // DH, v.shape[1] // DH
    ratio = vheads // kheads
    group = 2 if kheads % 2 == 0 else 1
    shapes = [(q, BF), (k, BF), (v, BF), (beta, F32), (gc, F32), (gr, F32)]
    square = (DH, DH)
    vmem = pl.BlockSpec(memory_space=pltpu.VMEM)
    return pl.pallas_call(
        functools.partial(core_kernel, kheads, ratio, group),
        out_shape=[jax.ShapeDtypeStruct(a.shape, kind) for a, kind in shapes],
        in_specs=[vmem] * 8,
        out_specs=[vmem] * 6,
        scratch_shapes=[
            pltpu.VMEM(q.shape, F32),
            pltpu.VMEM(k.shape, F32),
            pltpu.VMEM(v.shape, F32),
            pltpu.VMEM((size + 16, width), F32),
            pltpu.VMEM((size + 16, width), F32),
            pltpu.VMEM((size + 8, width), F32),
            pltpu.VMEM((16, width), BF),
            pltpu.VMEM((16, width), BF),
            pltpu.VMEM((8, width), F32),
            pltpu.SemaphoreType.DMA((4,)),
            pltpu.VMEM((vheads, size, size), BF),
            pltpu.VMEM((vheads, size, DH), BF),
            pltpu.VMEM((vheads, size, DH), F32),
            pltpu.VMEM((vheads, size, DH), F32),
            pltpu.VMEM((2, vheads) + square, BF),
            pltpu.VMEM((2, vheads) + square, F32),
            pltpu.VMEM((vheads, 8, DH), F32),
            pltpu.VMEM((2, vheads) + square, BF),
            pltpu.VMEM((2, vheads) + square, BF),
            pltpu.SemaphoreType.DMA((2, vheads)),
            pltpu.SemaphoreType.DMA((2, vheads)),
        ],
        compiler_params=pltpu.CompilerParams(
            collective_id=0, has_side_effects=True, vmem_limit_bytes=40 * 1024 * 1024
        ),
    )(q, k, v, taps, beta, gc, gr, grad_core)


def running_sum(log_decay):
    size = log_decay.shape[0]
    row = lax.broadcasted_iota(jnp.int32, (size, size), 0)
    col = lax.broadcasted_iota(jnp.int32, (size, size), 1)
    return jnp.dot(
        jnp.where(row >= col, 1.0, 0.0), log_decay, precision=lax.Precision.HIGHEST,
        preferred_element_type=F32,
    )


def local(
    inputs, query_weight, key_weight, value_weight, beta_weight, alpha_weight,
    query_filter, key_filter, value_filter, decay_log, step_bias, grad_core,
):
    weights = (query_weight, key_weight, value_weight, beta_weight, alpha_weight)
    pair = lax.axis_size("tp") == 2
    side = lax.axis_index("tp")
    if pair:
        other = lax.ppermute(inputs, "tp", [(0, 1), (1, 0)])
        whole = jnp.where(
            side == 0,
            jnp.concatenate([inputs, other], 1),
            jnp.concatenate([other, inputs], 1),
        )
    else:
        whole = lax.all_gather(inputs, "tp", axis=1, tiled=True)
    rounded = lax.optimization_barrier(
        tuple(jnp.dot(whole, w, preferred_element_type=F32).astype(BF) for w in weights)
    )
    taps = jnp.concatenate([query_filter, key_filter, value_filter], 1).astype(F32)

    def front(beta_raw, alpha_raw):
        beta = jax.nn.sigmoid(beta_raw)
        log_decay = -jnp.exp(decay_log) * jax.nn.softplus(alpha_raw + step_bias)
        return beta, running_sum(log_decay)

    (beta, gc), front_vjp = jax.vjp(front, rounded[3].astype(F32), rounded[4].astype(F32))
    dq, dk, dv, dbeta, dgc, dgr = recurrence_grads(
        *rounded[:3], taps, beta, gc, gc.T, grad_core
    )
    grads = front_vjp((dbeta, dgc + dgr.T))
    full = [dq, dk, dv] + [g.astype(BF) for g in grads]

    total = 0.0
    for grad_rows, weight in zip(full, weights):
        total = total + lax.dot_general(
            grad_rows, weight, (((1,), (1,)), ((), ())), preferred_element_type=F32
        )
    share = inputs.shape[1]
    if pair:
        far = lax.dynamic_slice_in_dim(total, (1 - side) * share, share, 1).astype(BF)
        arrived = lax.ppermute(far, "tp", [(0, 1), (1, 0)])
        near = lax.dynamic_slice_in_dim(total, side * share, share, 1)
        return (near + arrived.astype(F32)).astype(BF)
    return lax.psum_scatter(
        total.astype(BF), "tp", scatter_dimension=1, tiled=True
    )


def solution(mesh):
    return jax.shard_map(
        local,
        mesh=mesh,
        in_specs=(
            P("ctx", "tp"),
            P(None, "tp"),
            P(None, "tp"),
            P(None, "tp"),
            P(None, "tp"),
            P(None, "tp"),
            P(None, "tp"),
            P(None, "tp"),
            P(None, "tp"),
            P("tp"),
            P("tp"),
            P("ctx", "tp"),
        ),
        out_specs=P("ctx", "tp"),
        check_vma=False,
    )
```
